256 devices in a mesh: frame: 32 (over x, z_lo, core), patch: 8 (over z_hi, y).
Axes of the slice: x: 4, y: 4, z: 8 (z_hi: 2, z_lo: 4; z = z_hi * 4 + z_lo), core: 2. Of those that a mesh axis runs over, the one named last changes fastest.
Arguments:
- clip: bfloat16 [4, 32, 1024, 1280], P(None, 'frame', 'patch'), may hold values from -54 to 54
- norm_time: float32 [1280], replicated, may hold values from 0.1 to 1.9
- w_time_qkv: bfloat16 [1280, 1920], replicated, may hold values from -0.15625 to 0.15625
- q_gain_time: float32 [640], replicated, may hold values from 1 to 2
- k_gain_time: float32 [640], replicated, may hold values from 1 to 2
- w_time_out: bfloat16 [640, 1280], replicated, may hold values from -0.25 to 0.25
- norm_space: float32 [1280], replicated, may hold values from 0.1 to 1.9
- w_space_qkv: bfloat16 [1280, 1920], replicated, may hold values from -0.15625 to 0.15625
- q_gain_space: float32 [640], replicated, may hold values from 1 to 2
- k_gain_space: float32 [640], replicated, may hold values from 1 to 2
Outputs:
- spatial_out: bfloat16 [4, 32, 1024, 640], P(None, 'frame', 'patch')
The draws below stay inside these ranges and needn't reach their ends.
All inputs are finite; a program needn't handle non-finite values.
Results may differ from the reference program's by a relative error of at most 0.025.
Values may be sent and summed in bfloat16 or wider, within the bound.
A program may use at most 128 MiB of HBM per device.

```python
import math
import jax
import jax.numpy as jnp
from jax import lax

D = 1280
HEADS = 8
HDIM = 80
CLIPS = 4
FRAMES = 32
PATCHES = 1024


def draw_clip(key, part):
    key = jax.random.fold_in(key, 7)
    key_base = jax.random.fold_in(key, 1)
    key_rows = jax.random.fold_in(key, 2)
    key_cols = jax.random.fold_in(key, 3)
    full_shape = (CLIPS, FRAMES, PATCHES, D)
    low = math.log(0.3)
    high = math.log(3.0)
    row_scale = jnp.exp(jax.random.uniform(key_rows, (CLIPS, FRAMES, PATCHES, 1), jnp.float32, low, high))
    col_scale = jnp.exp(jax.random.uniform(key_cols, (D,), jnp.float32, low, high))
    base = jnp.clip(jax.random.normal(key_base, full_shape, jnp.float32), -6.0, 6.0)
    return (base * row_scale * col_scale).astype(jnp.bfloat16)


def noise(rng, shape, width, reach, kind=jnp.bfloat16):
    array = jax.random.normal(rng, shape, jnp.float32) * width
    return jnp.minimum(jnp.maximum(array, -reach), reach).astype(kind)


def setup_inputs(seed: int = 0) -> dict:
    seeds = jax.random.split(jax.random.key(seed), 11)
    clip = draw_clip(jax.random.fold_in(seeds[10], 71), 0)
    norm_time = jnp.clip(1.0 + 0.18 * jax.random.normal(seeds[1], (D,), jnp.float32), 0.1, 1.9)
    w_time_qkv = noise(seeds[2], (D, 3 * HEADS * HDIM), D ** -0.5, 0.15625)
    q_gain_time = jnp.clip(jax.random.uniform(seeds[3], (HEADS * HDIM,), jnp.float32, 1.0, 2.0), 1.0, 2.0)
    k_gain_time = jnp.clip(jax.random.uniform(seeds[4], (HEADS * HDIM,), jnp.float32, 1.0, 2.0), 1.0, 2.0)
    w_time_out = noise(seeds[5], (HEADS * HDIM, D), (HEADS * HDIM) ** -0.5, 0.25)
    norm_space = jnp.clip(1.0 + 0.18 * jax.random.normal(seeds[6], (D,), jnp.float32), 0.1, 1.9)
    w_space_qkv = noise(seeds[7], (D, 3 * HEADS * HDIM), D ** -0.5, 0.15625)
    q_gain_space = jnp.clip(jax.random.uniform(seeds[8], (HEADS * HDIM,), jnp.float32, 1.0, 2.0), 1.0, 2.0)
    k_gain_space = jnp.clip(jax.random.uniform(seeds[9], (HEADS * HDIM,), jnp.float32, 1.0, 2.0), 1.0, 2.0)
    return dict(clip=clip, norm_time=norm_time, w_time_qkv=w_time_qkv, q_gain_time=q_gain_time, k_gain_time=k_gain_time, w_time_out=w_time_out, norm_space=norm_space, w_space_qkv=w_space_qkv, q_gain_space=q_gain_space, k_gain_space=k_gain_space)


epsilon = 1e-06

def layer_norm(token_rows, norm_gain):
    values = token_rows.astype(jnp.float32)
    average = lax.optimization_barrier(jnp.mean(values, axis=-1, keepdims=True))
    centred = values - average
    variance = lax.optimization_barrier(jnp.mean(centred * centred, axis=-1, keepdims=True))
    return (centred * lax.rsqrt(variance + epsilon) * norm_gain).astype(jnp.bfloat16)

def head_norm(projected, head_gain, head_size):
    leading = projected.shape[:-1]
    split_heads = projected.reshape(leading + (projected.shape[-1] // head_size, head_size))
    squares = lax.optimization_barrier(jnp.mean(split_heads * split_heads, axis=-1, keepdims=True))
    scaled = split_heads * lax.rsqrt(squares + epsilon)
    return (scaled.reshape(projected.shape) * head_gain).astype(jnp.bfloat16)

def project_heads(normed, weight, query_gain, key_gain, head_size):
    inner_width = weight.shape[1] // 3
    product = jnp.dot(normed, weight, preferred_element_type=jnp.float32)
    query = head_norm(product[:, :inner_width], query_gain, head_size)
    keys = head_norm(product[:, inner_width:2 * inner_width], key_gain, head_size)
    values = product[:, 2 * inner_width:].astype(jnp.bfloat16)
    return (query, keys, values)

def time_attention(query, keys, values):
    clip_count, frame_count, patch_count, inner_width = query.shape
    split = (clip_count, frame_count, patch_count, inner_width // HDIM, HDIM)
    query_heads = query.reshape(split).astype(jnp.float32)
    key_heads = keys.reshape(split).astype(jnp.float32)
    value_heads = values.reshape(split).astype(jnp.float32)
    scores = jnp.einsum('cfphd,cgphd->cphfg', query_heads, key_heads) * HDIM ** (-0.5)
    exponent = jnp.exp(scores)
    totals = lax.optimization_barrier(jnp.sum(exponent, axis=-1))
    rounded = lax.optimization_barrier(exponent.astype(jnp.bfloat16))
    summed = jnp.einsum('cphfg,cgphd->cfphd', rounded.astype(jnp.float32), value_heads)
    result = summed / jnp.transpose(totals, (0, 3, 1, 2))[..., None]
    return result.reshape(query.shape).astype(jnp.bfloat16)

def space_frame(inputs):
    query, keys, values = inputs
    patch_count, inner_width = query.shape
    split = (patch_count, inner_width // HDIM, HDIM)
    query_heads = query.reshape(split).astype(jnp.float32)
    key_heads = keys.reshape(split).astype(jnp.float32)
    value_heads = values.reshape(split).astype(jnp.float32)
    scores = jnp.einsum('qhd,khd->hqk', query_heads, key_heads) * HDIM ** (-0.5)
    exponent = jnp.exp(scores)
    totals = lax.optimization_barrier(jnp.sum(exponent, axis=-1))
    rounded = lax.optimization_barrier(exponent.astype(jnp.bfloat16))
    summed = jnp.einsum('hqk,khd->qhd', rounded.astype(jnp.float32), value_heads)
    result = summed / jnp.transpose(totals, (1, 0))[..., None]
    return result.reshape(query.shape).astype(jnp.bfloat16)

def reference(clip, norm_time, w_time_qkv, q_gain_time, k_gain_time, w_time_out, norm_space, w_space_qkv, q_gain_space, k_gain_space):
    inner_width = w_time_out.shape[0]
    token_rows = clip.reshape(-1, D)
    normed = layer_norm(token_rows, norm_time)
    query, keys, values = project_heads(normed, w_time_qkv, q_gain_time, k_gain_time, HDIM)
    attn_shape = (CLIPS, FRAMES, PATCHES, inner_width)
    attended = time_attention(query.reshape(attn_shape), keys.reshape(attn_shape), values.reshape(attn_shape))
    delta = jnp.dot(attended.reshape(-1, inner_width), w_time_out, preferred_element_type=jnp.float32)
    mixed = (token_rows.astype(jnp.float32) + delta).astype(jnp.bfloat16)
    space_normed = layer_norm(mixed, norm_space)
    space_query, space_keys, space_values = project_heads(space_normed, w_space_qkv, q_gain_space, k_gain_space, HDIM)
    frame_shape = (CLIPS * FRAMES, PATCHES, inner_width)
    spatial = lax.map(space_frame, (space_query.reshape(frame_shape), space_keys.reshape(frame_shape), space_values.reshape(frame_shape)))
    return spatial.reshape(attn_shape)
```

```python
import math

import jax
import jax.numpy as jnp
from jax import lax
from jax.experimental import pallas as pl
from jax.experimental.pallas import tpu as pltpu
from jax.sharding import PartitionSpec as P

MESH = pl.DeviceIdType.MESH
HDIM = 80
HEADS = 8
D = 1280
INNER = 640
HALF = 384
EPS = 1e-06
SCALE = HDIM ** (-0.5) * math.log2(math.e)
BF = jnp.bfloat16
F32 = jnp.float32
WINDOWS = (0, 0, 128, 128, 256, 256, 384, 384)


def div(a, b):
    return lax.div(a, jnp.int32(b))


def rem(a, b):
    return lax.rem(a, jnp.int32(b))


def kernel(
    clip, norm_t, w_tqkv, qg_t, kg_t, w_out, norm_s, w_sqkv, qg_s, kg_s,
    out,
    wt, wo, ws, blocks, pmask, tok, tq, tk, tv, mixed, tok2, send_qkv, qkv, vm, att, home,
    wsem, s1, r1, s2, r2, sq, rq, s4, r4,
):
    frame, patch = lax.axis_index("frame"), lax.axis_index("patch")
    x, zl, core = div(frame, 8), rem(div(frame, 2), 4), rem(frame, 2)
    zh, y = div(patch, 4), rem(patch, 4)
    z = zh * 4 + zl
    c, zb = div(z, 2), rem(z, 2)

    def flip(zz, cc):
        return rem(zz + 1 + rem(div(cc + 1, 2), 2), 2)

    zh_src = flip(zb, c)
    pg_src = zh_src * 4 + y

    def is_me(device):
        return (device[0] == frame) & (device[1] == patch)

    def not_me(device):
        return (device[0] != frame) | (device[1] != patch)

    def target1(i):
        xt = rem(x + div(i, 8), 4)
        ct = rem(c + 1 + i, 4)
        kt = rem(div(i, 4), 2)
        zt = 2 * ct + flip(zh, ct)
        return (xt * 8 + rem(zt, 4) * 2 + kt, div(zt, 4) * 4 + y), ct, kt * 4 + xt

    def source1(i):
        return (i, pg_src)

    def target2(f):
        zt = 2 * c + rem(f, 2)
        return (div(f, 8) * 8 + rem(zt, 4) * 2 + core, div(zt, 4) * 4 + rem(div(f, 2), 4))

    def source2(i):
        zs = 2 * c + rem(i, 2)
        return (div(i, 8) * 8 + rem(zs, 4) * 2 + core, div(zs, 4) * 4 + rem(div(i, 2), 4))

    home_frame = x * 8 + y * 2 + zb

    def target4(g):
        return (home_frame, g)

    def source4(i):
        zs = 2 * div(i, 2) + core
        return (x * 8 + rem(zs, 4) * 2 + rem(i, 2), div(zs, 4) * 4 + zl)

    partner = (x * 8 + zl * 2 + 1 - core, patch)

    loads = (
        pltpu.make_async_copy(w_tqkv, wt, wsem.at[0]),
        pltpu.make_async_copy(w_out, wo, wsem.at[1]),
        pltpu.make_async_copy(w_sqkv, ws, wsem.at[2]),
    )
    loads[0].start()
    loads[1].start()
    loads[2].start()

    barrier = pltpu.get_barrier_semaphore()

    def greet(device):
        @pl.when(not_me(device))
        def _():
            pl.semaphore_signal(barrier, inc=1, device_id=device, device_id_type=MESH)

    def greet1(i, carry):
        greet(source1(rem(frame + i, 32)))
        return carry

    def greet2(i, carry):
        greet(source2(i))
        return carry

    def greet4(i, carry):
        greet(source4(i))
        return carry

    lax.fori_loop(0, 32, greet1, 0)
    lax.fori_loop(0, 32, greet2, 0)
    lax.fori_loop(0, 8, greet4, 0)
    greet(partner)

    rows = lax.broadcasted_iota(jnp.int32, (INNER, INNER), 0)
    cols = lax.broadcasted_iota(jnp.int32, (INNER, INNER), 1)
    head_of = lambda v: lax.shift_right_logical(v * 52429, 22)
    blocks[...] = jnp.where(head_of(rows) == head_of(cols), 1.0, 0.0).astype(BF)
    rows = lax.broadcasted_iota(jnp.int32, (128, 512), 0)
    cols = lax.broadcasted_iota(jnp.int32, (128, 512), 1)
    pmask[...] = jnp.where((rows & 15) == (cols & 15), 1.0, 0.0).astype(BF)

    own1 = jnp.where(zh_src == zh, 1, 0)
    own4 = jnp.where((core == zb) & (zl == y), 1, 0)
    pl.semaphore_wait(barrier, 32 - own1 + 31 + 8 - own4 + 1)

    def copy1(i):
        device, ct, b = target1(i)
        src = clip.at[ct, 0, pl.ds(pl.multiple_of(b * 16, 16), 16)]
        return device, src

    def send1(i, carry):
        device, src = copy1(i)

        @pl.when(not_me(device))
        def _():
            pltpu.make_async_remote_copy(
                src_ref=src, dst_ref=tok.at[frame], send_sem=s1.at[i], recv_sem=r1.at[frame],
                device_id=device, device_id_type=MESH,
            ).start()

        @pl.when(is_me(device))
        def _():
            pltpu.make_async_copy(src, tok.at[frame], r1.at[frame]).start()

        return carry

    lax.fori_loop(0, 32, send1, 0)

    def layer_norm(values, gain):
        average = jnp.mean(values, axis=-1, keepdims=True)
        centred = values - average
        variance = jnp.mean(centred * centred, axis=-1, keepdims=True)
        return (centred * lax.rsqrt(variance + EPS) * gain).astype(BF)

    def head_norm(part, gain):
        squares = jnp.dot((part * part).astype(BF), blocks[...], preferred_element_type=F32)
        return (part * lax.rsqrt(squares * (1.0 / HDIM) + EPS) * gain).astype(BF)

    def project(values, norm, weight, q_gain, k_gain):
        normed = layer_norm(values, norm[...])
        product = jnp.dot(normed, weight[...], preferred_element_type=F32)
        query = head_norm(product[:, :INNER], q_gain[...])
        keys = head_norm(product[:, INNER : 2 * INNER], k_gain[...])
        return query, keys, product[:, 2 * INNER :].astype(BF)

    def wait_local(src, dst, sem):
        pltpu.make_async_copy(src, dst, sem).wait()

    loads[0].wait()

    def time_project(j, carry):
        xs = rem(x + j, 4)

        def wait(i, inner):
            slot = xs * 8 + i
            wait_local(tok.at[slot], tok.at[slot], r1.at[slot])
            return inner

        lax.fori_loop(0, 8, wait, 0)
        values = tok[pl.ds(xs * 8, 8)].reshape(128, D).astype(F32)
        query, keys, vals = project(values, norm_t, wt, qg_t, kg_t)
        tq[xs] = query
        at = pl.ds(pl.multiple_of(xs * 128, 128), 128)
        tk[at, :] = keys
        tv[at, :] = vals
        return carry

    lax.fori_loop(0, 4, time_project, 0)
    loads[1].wait()

    lane = lax.broadcasted_iota(jnp.int32, (1, 256), 1)

    def time_attend(j, carry):
        xs = rem(x + 1 + j, 4)
        tiles = [jnp.zeros((128, 128), F32)] * 5
        for h in range(HEADS):
            w = WINDOWS[h]
            first = h * HDIM - w
            mask = (lane >= first) & (lane < first + HDIM)
            spare = 255 if first + HDIM <= 255 else 0
            query = jnp.where(mask, tq[xs, :, w : w + 256], 0.0).astype(BF)
            scores = lax.dot_general(
                query, tk[:, w : w + 256], (((1,), (1,)), ((), ())), preferred_element_type=F32
            )
            prob = jnp.exp2(scores * SCALE).astype(BF) * pmask[...]
            vals = jnp.where(mask, tv[:, w : w + 256], 1.0).astype(BF)
            summed = jnp.dot(prob, vals, preferred_element_type=F32)
            result = summed * (1.0 / summed[:, spare : spare + 1])
            t = w // 128
            tiles[t] = jnp.where(mask[:, :128], result[:, :128], tiles[t])
            tiles[t + 1] = jnp.where(mask[:, 128:], result[:, 128:], tiles[t + 1])
        attended = jnp.concatenate([tile.astype(BF) for tile in tiles], axis=1)
        delta = jnp.dot(attended, wo[...], preferred_element_type=F32)
        values = tok[pl.ds(xs * 8, 8)].reshape(128, D).astype(F32)
        mixed[pl.ds(xs * 8, 8)] = (values + delta).astype(BF).reshape(8, 16, D)

        def send(i, inner):
            f = xs * 8 + i
            device = target2(f)
            slot = x * 8 + pg_src

            @pl.when(not_me(device))
            def _():
                pltpu.make_async_remote_copy(
                    src_ref=mixed.at[f], dst_ref=tok2.at[slot], send_sem=s2.at[f],
                    recv_sem=r2.at[slot], device_id=device, device_id_type=MESH,
                ).start()

            @pl.when(is_me(device))
            def _():
                pltpu.make_async_copy(mixed.at[f], tok2.at[slot], r2.at[slot]).start()

            return inner

        lax.fori_loop(0, 8, send, 0)
        return carry

    lax.fori_loop(0, 4, time_attend, 0)
    loads[2].wait()

    def exchange(xs):
        return pltpu.make_async_remote_copy(
            src_ref=send_qkv.at[xs], dst_ref=qkv.at[core, xs], send_sem=sq.at[xs],
            recv_sem=rq.at[xs], device_id=partner, device_id_type=MESH,
        )

    def space_project(j, carry):
        xs = rem(x + 3 - j, 4)

        def wait(i, inner):
            slot = xs * 8 + i
            wait_local(tok2.at[slot], tok2.at[slot], r2.at[slot])
            return inner

        lax.fori_loop(0, 8, wait, 0)
        values = tok2[pl.ds(xs * 8, 8)].reshape(128, D).astype(F32)
        parts = project(values, norm_s, ws, qg_s, kg_s)
        for n in range(3):
            low, high = parts[n][:, :HALF], parts[n][:, INNER - HALF :]
            qkv[core, xs, n] = jnp.where(core == 0, low, high).reshape(8, 16, HALF)
            send_qkv[xs, n] = jnp.where(core == 0, high, low).reshape(8, 16, HALF)
        exchange(xs).start()
        return carry

    lax.fori_loop(0, 4, space_project, 0)

    def wait_partner(xs, carry):
        wait_local(send_qkv.at[xs], qkv.at[1 - core, xs], rq.at[xs])
        return carry

    lax.fori_loop(0, 4, wait_partner, 0)

    def head_mask(j):
        first = j * HDIM + 64 * core - (0 if j < 2 else 128)
        return (lane >= first) & (lane < first + HDIM)

    for j in range(4):
        w = 0 if j < 2 else 128
        vals = qkv[:, :, 2, :, :, w : w + 256].reshape(1024, 256)
        vm[j] = jnp.where(head_mask(j), vals, 1.0).astype(BF)

    def send4(g):
        device = target4(g)
        slot = c * 2 + core
        src, dst = att.at[g], home.at[slot]

        @pl.when(not_me(device))
        def _():
            pltpu.make_async_remote_copy(
                src_ref=src, dst_ref=dst, send_sem=s4.at[g], recv_sem=r4.at[slot],
                device_id=device, device_id_type=MESH,
            ).start()

        @pl.when(is_me(device))
        def _():
            pltpu.make_async_copy(src, dst, r4.at[slot]).start()

    def space_attend(j, carry):
        t = rem(zl + j, 4)
        tiles = [jnp.zeros((256, 128), F32)] * 3
        for h in range(4):
            w = 0 if h < 2 else 128
            spare = 255 if h < 2 else 0
            mask = head_mask(h)
            query = qkv[:, :, 0, pl.ds(2 * t, 2), :, w : w + 256].reshape(256, 256)
            query = jnp.where(mask, query, 0.0).astype(BF)
            keys = qkv[:, :, 1, :, :, w : w + 256].reshape(1024, 256)
            scores = lax.dot_general(
                query, keys, (((1,), (1,)), ((), ())), preferred_element_type=F32
            )
            prob = jnp.exp2(scores * SCALE).astype(BF)
            summed = jnp.dot(prob, vm[h], preferred_element_type=F32)
            result = summed * (1.0 / summed[:, spare : spare + 1])
            n = w // 128
            tiles[n] = jnp.where(mask[:, :128], result[:, :128], tiles[n])
            tiles[n + 1] = jnp.where(mask[:, 128:], result[:, 128:], tiles[n + 1])
        for n in range(3):
            tile = tiles[n].astype(BF).reshape(8, 2, 16, 128)
            for g in range(2):
                att[2 * t + g, :, :, n * 128 : (n + 1) * 128] = tile[:, g]
        send4(2 * t)
        send4(2 * t + 1)
        return carry

    lax.fori_loop(0, 4, space_attend, 0)

    def finish(i, carry):
        wait_local(home.at[2 * i], home.at[2 * i], r4.at[2 * i])
        wait_local(home.at[2 * i + 1], home.at[2 * i + 1], r4.at[2 * i + 1])
        low, high = home[2 * i].reshape(128, HALF), home[2 * i + 1].reshape(128, HALF)
        out[i, 0, :, :256] = low[:, :256]
        out[i, 0, :, 256:384] = low[:, 256:] + high[:, :128]
        out[i, 0, :, 384:] = high[:, 128:]
        return carry

    lax.fori_loop(0, 4, finish, 0)

    def done1(i, carry):
        device, src = copy1(i)

        @pl.when(not_me(device))
        def _():
            pltpu.make_async_remote_copy(
                src_ref=src, dst_ref=tok.at[frame], send_sem=s1.at[i], recv_sem=r1.at[frame],
                device_id=device, device_id_type=MESH,
            ).wait_send()

        return carry

    def done2(f, carry):
        device = target2(f)

        @pl.when(not_me(device))
        def _():
            pltpu.make_async_remote_copy(
                src_ref=mixed.at[f], dst_ref=tok2.at[f], send_sem=s2.at[f], recv_sem=r2.at[f],
                device_id=device, device_id_type=MESH,
            ).wait_send()

        return carry

    def done3(xs, carry):
        exchange(xs).wait_send()
        return carry

    def done4(g, carry):
        device = target4(g)

        @pl.when(not_me(device))
        def _():
            pltpu.make_async_remote_copy(
                src_ref=att.at[g], dst_ref=home.at[0], send_sem=s4.at[g], recv_sem=r4.at[0],
                device_id=device, device_id_type=MESH,
            ).wait_send()

        return carry

    lax.fori_loop(0, 32, done1, 0)
    lax.fori_loop(0, 32, done2, 0)
    lax.fori_loop(0, 4, done3, 0)
    lax.fori_loop(0, 8, done4, 0)


def body(
    clip, norm_time, w_time_qkv, q_gain_time, k_gain_time, w_time_out,
    norm_space, w_space_qkv, q_gain_space, k_gain_space,
):
    anywhere = pl.BlockSpec(memory_space=pl.ANY)
    vmem = pl.BlockSpec(memory_space=pltpu.VMEM)
    dma = pltpu.SemaphoreType.DMA
    flat = lambda gain: gain.reshape(1, -1)
    return pl.pallas_call(
        kernel,
        out_shape=jax.ShapeDtypeStruct((4, 1, 128, INNER), BF),
        in_specs=[anywhere, vmem, anywhere, vmem, vmem, anywhere, vmem, anywhere, vmem, vmem],
        out_specs=vmem,
        scratch_shapes=[
            pltpu.VMEM((D, 3 * INNER), BF),
            pltpu.VMEM((INNER, D), BF),
            pltpu.VMEM((D, 3 * INNER), BF),
            pltpu.VMEM((INNER, INNER), BF),
            pltpu.VMEM((128, 512), BF),
            pltpu.VMEM((32, 16, D), BF),
            pltpu.VMEM((4, 128, INNER), BF),
            pltpu.VMEM((512, INNER), BF),
            pltpu.VMEM((512, INNER), BF),
            pltpu.VMEM((32, 16, D), BF),
            pltpu.VMEM((32, 16, D), BF),
            pltpu.VMEM((4, 3, 8, 16, HALF), BF),
            pltpu.VMEM((2, 4, 3, 8, 16, HALF), BF),
            pltpu.VMEM((4, 1024, 256), BF),
            pltpu.VMEM((8, 8, 16, HALF), BF),
            pltpu.VMEM((8, 8, 16, HALF), BF),
            dma((3,)),
            dma((32,)), dma((32,)),
            dma((32,)), dma((32,)),
            dma((4,)), dma((4,)),
            dma((8,)), dma((8,)),
        ],
        compiler_params=pltpu.CompilerParams(
            collective_id=0, has_side_effects=True, vmem_limit_bytes=58 * 2**20
        ),
        cost_estimate=pl.CostEstimate(
            flops=2 * 512 * D * (6 * INNER + INNER), bytes_accessed=14 * 2**20, transcendentals=6 * 2**20
        ),
    )(
        clip, flat(norm_time), w_time_qkv, flat(q_gain_time), flat(k_gain_time), w_time_out,
        flat(norm_space), w_space_qkv, flat(q_gain_space), flat(k_gain_space),
    )


def solution(mesh):
    in_specs = (P(None, "frame", "patch", None),) + (P(),) * 9
    out_specs = P(None, "frame", "patch", None)
    return jax.shard_map(body, mesh=mesh, in_specs=in_specs, out_specs=out_specs, check_vma=False)
```

```python
import math

import jax
import jax.numpy as jnp
from jax import lax
from jax.experimental import pallas as pl
from jax.experimental.pallas import tpu as pltpu
from jax.sharding import PartitionSpec as P

MESH = pl.DeviceIdType.MESH
HDIM = 80
HEADS = 8
D = 1280
INNER = 640
HALF = 384
EPS = 1e-06
SCALE = HDIM ** (-0.5) * math.log2(math.e)
BF = jnp.bfloat16
F32 = jnp.float32
WINDOWS = (0, 0, 128, 128, 256, 256, 384, 384)


def div(a, b):
    return lax.div(a, jnp.int32(b))


def rem(a, b):
    return lax.rem(a, jnp.int32(b))


def kernel(
    clip, norm_t, w_tqkv, qg_t, kg_t, w_out, norm_s, w_sqkv, qg_s, kg_s,
    out,
    wt, wo, ws, blocks, pmask, swap, tok, tq, tk, tv, tatt, mixed, tok2, send_qkv, qkv, vm, att, home,
    wsem, s1, r1, s2, r2, sq, rq, s4, r4,
):
    frame, patch = lax.axis_index("frame"), lax.axis_index("patch")
    x, zl, core = div(frame, 8), rem(div(frame, 2), 4), rem(frame, 2)
    zh, y = div(patch, 4), rem(patch, 4)
    z = zh * 4 + zl
    c, zb = div(z, 2), rem(z, 2)

    def flip(zz, cc):
        return rem(zz + 1 + rem(div(cc + 1, 2), 2), 2)

    zh_src = flip(zb, c)
    pg_src = zh_src * 4 + y

    def is_me(device):
        return (device[0] == frame) & (device[1] == patch)

    def not_me(device):
        return (device[0] != frame) | (device[1] != patch)

    def target1(i):
        xt = rem(x + div(i, 8), 4)
        ct = rem(c + 1 + i, 4)
        kt = rem(div(i, 4), 2)
        zt = 2 * ct + flip(zh, ct)
        return (xt * 8 + rem(zt, 4) * 2 + kt, div(zt, 4) * 4 + y), ct, kt * 4 + xt

    def source1(i):
        return (i, pg_src)

    def target2(f):
        zt = 2 * c + rem(f, 2)
        yt = rem(div(f, 2) + zt, 4)
        return (div(f, 8) * 8 + rem(zt, 4) * 2 + core, div(zt, 4) * 4 + yt)

    def source2(i):
        zs = 2 * c + rem(i, 2)
        return (div(i, 8) * 8 + rem(zs, 4) * 2 + core, div(zs, 4) * 4 + rem(div(i, 2), 4))

    home_zl = rem(y + 8 - z, 4)
    home_frame = x * 8 + home_zl * 2 + zb

    def target4(g):
        return (home_frame, g)

    def source4(i):
        zs = 2 * div(i, 2) + core
        return (x * 8 + rem(zs, 4) * 2 + rem(i, 2), div(zs, 4) * 4 + rem(zl + zs, 4))

    partner = (x * 8 + zl * 2 + 1 - core, patch)

    loads = (
        pltpu.make_async_copy(w_tqkv, wt, wsem.at[0]),
        pltpu.make_async_copy(w_out, wo, wsem.at[1]),
        pltpu.make_async_copy(w_sqkv, ws, wsem.at[2]),
    )
    loads[0].start()
    loads[1].start()
    loads[2].start()

    barrier = pltpu.get_barrier_semaphore()

    def greet(device):
        @pl.when(not_me(device))
        def _():
            pl.semaphore_signal(barrier, inc=1, device_id=device, device_id_type=MESH)

    def greet1(i, carry):
        greet(source1(rem(frame + i, 32)))
        return carry

    def greet2(i, carry):
        greet(source2(i))
        return carry

    def greet4(i, carry):
        greet(source4(i))
        return carry

    lax.fori_loop(0, 32, greet1, 0)
    lax.fori_loop(0, 32, greet2, 0)
    lax.fori_loop(0, 8, greet4, 0)
    greet(partner)

    rows = lax.broadcasted_iota(jnp.int32, (INNER, INNER), 0)
    cols = lax.broadcasted_iota(jnp.int32, (INNER, INNER), 1)
    head_of = lambda v: lax.shift_right_logical(v * 52429, 22)
    blocks[...] = jnp.where(head_of(rows) == head_of(cols), 1.0, 0.0).astype(BF)
    rows = lax.broadcasted_iota(jnp.int32, (128, 128), 0)
    cols = lax.broadcasted_iota(jnp.int32, (128, 128), 1)
    pmask[...] = jnp.where((rows >> 5) == (cols >> 5), 1.0, 0.0).astype(BF)
    swap[...] = jnp.where(cols == (rows & 7) * 16 + (rows >> 3), 1.0, 0.0).astype(BF)

    own1 = jnp.where(zh_src == zh, 1, 0)
    own4 = jnp.where(home_frame == frame, 1, 0)
    pl.semaphore_wait(barrier, 32 - own1 + 31 + 8 - own4 + 1)

    def copy1(i):
        device, ct, b = target1(i)
        src = clip.at[ct, 0, pl.ds(pl.multiple_of(b * 16, 16), 16)]
        return device, src

    def send1(i, carry):
        device, src = copy1(i)

        @pl.when(not_me(device))
        def _():
            pltpu.make_async_remote_copy(
                src_ref=src, dst_ref=tok.at[frame], send_sem=s1.at[i], recv_sem=r1.at[frame],
                device_id=device, device_id_type=MESH,
            ).start()

        @pl.when(is_me(device))
        def _():
            pltpu.make_async_copy(src, tok.at[frame], r1.at[frame]).start()

        return carry

    lax.fori_loop(0, 32, send1, 0)

    def layer_norm(values, gain):
        average = jnp.mean(values, axis=-1, keepdims=True)
        centred = values - average
        variance = jnp.mean(centred * centred, axis=-1, keepdims=True)
        return (centred * lax.rsqrt(variance + EPS) * gain).astype(BF)

    def head_norm(part, gain):
        squares = jnp.dot((part * part).astype(BF), blocks[...], preferred_element_type=F32)
        return (part * lax.rsqrt(squares * (1.0 / HDIM) + EPS) * gain).astype(BF)

    def project(values, norm, weight, q_gain, k_gain):
        normed = layer_norm(values, norm[...])
        product = jnp.dot(normed, weight[...], preferred_element_type=F32)
        query = head_norm(product[:, :INNER], q_gain[...])
        keys = head_norm(product[:, INNER : 2 * INNER], k_gain[...])
        return query, keys, product[:, 2 * INNER :].astype(BF)

    def wait_local(src, dst, sem):
        pltpu.make_async_copy(src, dst, sem).wait()

    loads[0].wait()

    def time_project(j, carry):
        xs = rem(x + j, 4)

        def wait(i, inner):
            slot = xs * 8 + i
            wait_local(tok.at[slot], tok.at[slot], r1.at[slot])
            return inner

        lax.fori_loop(0, 8, wait, 0)
        values = jnp.dot(
            swap[...], tok[pl.ds(xs * 8, 8)].reshape(128, D), preferred_element_type=F32
        )
        parts = project(values, norm_t, wt, qg_t, kg_t)
        at = pl.ds(pl.multiple_of(xs * 8, 8), 8)
        for ref, part in zip((tq, tk, tv), parts):
            ref[:, at, :] = part.astype(F32).reshape(16, 8, INNER)
        return carry

    lax.fori_loop(0, 4, time_project, 0)
    loads[1].wait()

    lane = lax.broadcasted_iota(jnp.int32, (1, 256), 1)

    def time_attend(g, carry):
        at = pl.ds(4 * g, 4)
        tiles = [jnp.zeros((128, 128), F32)] * 5
        for h in range(HEADS):
            w = WINDOWS[h]
            first = h * HDIM - w
            mask = (lane >= first) & (lane < first + HDIM)
            spare = 255 if first + HDIM <= 255 else 0
            query = jnp.where(mask, tq[at, :, w : w + 256].reshape(128, 256), 0.0).astype(BF)
            keys = tk[at, :, w : w + 256].reshape(128, 256).astype(BF)
            scores = lax.dot_general(
                query, keys, (((1,), (1,)), ((), ())), preferred_element_type=F32
            )
            prob = jnp.exp2(scores * SCALE).astype(BF) * pmask[...]
            vals = jnp.where(mask, tv[at, :, w : w + 256].reshape(128, 256), 1.0).astype(BF)
            summed = jnp.dot(prob, vals, preferred_element_type=F32)
            result = summed * (1.0 / summed[:, spare : spare + 1])
            t = w // 128
            tiles[t] = jnp.where(mask[:, :128], result[:, :128], tiles[t])
            tiles[t + 1] = jnp.where(mask[:, 128:], result[:, 128:], tiles[t + 1])
        rows = pl.ds(pl.multiple_of(g * 128, 128), 128)
        for n in range(5):
            tatt[rows, n * 128 : (n + 1) * 128] = tiles[n].astype(BF)
        return carry

    lax.fori_loop(0, 4, time_attend, 0)

    def time_mix(j, carry):
        zls = [rem(x + j + 4 - a, 4) for a in range(4)]
        first = [a * 8 + zls[a] * 2 for a in range(4)]
        parts = []
        for a in range(4):
            rows = lax.broadcasted_iota(jnp.int32, (32, 512), 0)
            cols = lax.broadcasted_iota(jnp.int32, (32, 512), 1)
            parts.append(cols == (rows & 15) * 32 + (rows >> 4) + first[a])
        pick = jnp.concatenate([jnp.where(part, 1.0, 0.0).astype(BF) for part in parts], axis=0)
        attended = jnp.dot(pick, tatt[...], preferred_element_type=F32).astype(BF)
        delta = jnp.dot(attended, wo[...], preferred_element_type=F32)
        for a in range(4):
            values = tok[pl.ds(first[a], 2)].reshape(32, D).astype(F32)
            total = (values + delta[32 * a : 32 * a + 32]).astype(BF)
            mixed[pl.ds(first[a], 2)] = total.reshape(2, 16, D)

        def send(i, inner):
            a = rem(x + 1 + i, 4)
            f = a * 8 + rem(x + j + 4 - a, 4) * 2 + div(i, 4)
            device = target2(f)
            slot = x * 8 + pg_src

            @pl.when(not_me(device))
            def _():
                pltpu.make_async_remote_copy(
                    src_ref=mixed.at[f], dst_ref=tok2.at[slot], send_sem=s2.at[f],
                    recv_sem=r2.at[slot], device_id=device, device_id_type=MESH,
                ).start()

            @pl.when(is_me(device))
            def _():
                pltpu.make_async_copy(mixed.at[f], tok2.at[slot], r2.at[slot]).start()

            return inner

        lax.fori_loop(0, 8, send, 0)
        return carry

    lax.fori_loop(0, 4, time_mix, 0)
    loads[2].wait()

    def exchange(xs):
        return pltpu.make_async_remote_copy(
            src_ref=send_qkv.at[xs], dst_ref=qkv.at[core, xs], send_sem=sq.at[xs],
            recv_sem=rq.at[xs], device_id=partner, device_id_type=MESH,
        )

    def space_project(j, carry):
        xs = rem(x + home_zl + 4 - j, 4)

        def wait(i, inner):
            slot = xs * 8 + i
            wait_local(tok2.at[slot], tok2.at[slot], r2.at[slot])
            return inner

        lax.fori_loop(0, 8, wait, 0)
        values = tok2[pl.ds(xs * 8, 8)].reshape(128, D).astype(F32)
        parts = project(values, norm_s, ws, qg_s, kg_s)
        for n in range(3):
            low, high = parts[n][:, :HALF], parts[n][:, INNER - HALF :]
            qkv[core, xs, n] = jnp.where(core == 0, low, high).reshape(8, 16, HALF)
            send_qkv[xs, n] = jnp.where(core == 0, high, low).reshape(8, 16, HALF)
        exchange(xs).start()
        return carry

    lax.fori_loop(0, 4, space_project, 0)

    def wait_partner(xs, carry):
        wait_local(send_qkv.at[xs], qkv.at[1 - core, xs], rq.at[xs])
        return carry

    lax.fori_loop(0, 4, wait_partner, 0)

    def head_mask(j):
        first = j * HDIM + 64 * core - (0 if j < 2 else 128)
        return (lane >= first) & (lane < first + HDIM)

    for j in range(4):
        w = 0 if j < 2 else 128
        vals = qkv[:, :, 2, :, :, w : w + 256].reshape(1024, 256)
        vm[j] = jnp.where(head_mask(j), vals, 1.0).astype(BF)

    def send4(g):
        device = target4(g)
        slot = c * 2 + core
        src, dst = att.at[g], home.at[slot]

        @pl.when(not_me(device))
        def _():
            pltpu.make_async_remote_copy(
                src_ref=src, dst_ref=dst, send_sem=s4.at[g], recv_sem=r4.at[slot],
                device_id=device, device_id_type=MESH,
            ).start()

        @pl.when(is_me(device))
        def _():
            pltpu.make_async_copy(src, dst, r4.at[slot]).start()

    def space_attend(j, carry):
        t = rem(zl + j, 4)
        tiles = [jnp.zeros((256, 128), F32)] * 3
        for h in range(4):
            w = 0 if h < 2 else 128
            spare = 255 if h < 2 else 0
            mask = head_mask(h)
            query = qkv[:, :, 0, pl.ds(2 * t, 2), :, w : w + 256].reshape(256, 256)
            query = jnp.where(mask, query, 0.0).astype(BF)
            keys = qkv[:, :, 1, :, :, w : w + 256].reshape(1024, 256)
            scores = lax.dot_general(
                query, keys, (((1,), (1,)), ((), ())), preferred_element_type=F32
            )
            prob = jnp.exp2(scores * SCALE).astype(BF)
            summed = jnp.dot(prob, vm[h], preferred_element_type=F32)
            result = summed * (1.0 / summed[:, spare : spare + 1])
            n = w // 128
            tiles[n] = jnp.where(mask[:, :128], result[:, :128], tiles[n])
            tiles[n + 1] = jnp.where(mask[:, 128:], result[:, 128:], tiles[n + 1])
        first = core == 0
        whole = [jnp.where(first, tiles[n], tiles[n + 1]).astype(BF) for n in range(2)]
        shared = jnp.where(first, tiles[2], tiles[0])
        packed = shared[:128] + pltpu.roll(shared[128:], 64, 1)
        packed = packed.astype(BF).reshape(4, 2, 16, 128)
        for g in range(2):
            for n in range(2):
                att[2 * t + g, 8 * n : 8 * n + 8] = whole[n].reshape(8, 2, 16, 128)[:, g]
            att[2 * t + g, 16:] = packed[:, g]
        send4(2 * t)
        send4(2 * t + 1)
        return carry

    lax.fori_loop(0, 4, space_attend, 0)

    def finish(i, carry):
        wait_local(home.at[2 * i], home.at[2 * i], r4.at[2 * i])
        wait_local(home.at[2 * i + 1], home.at[2 * i + 1], r4.at[2 * i + 1])
        for half in range(2):
            for n in range(2):
                at = (3 * half + n) * 128
                out[i, 0, :, at : at + 128] = home[2 * i + half, 8 * n : 8 * n + 8].reshape(128, 128)
        low = home[2 * i, 16:].reshape(64, 128).astype(F32)
        high = home[2 * i + 1, 16:].reshape(64, 128).astype(F32)
        left = lane[:, :128] < 64
        out[i, 0, :64, 256:384] = jnp.where(left, low, high).astype(BF)
        out[i, 0, 64:, 256:384] = pltpu.roll(jnp.where(left, high, low), 64, 1).astype(BF)
        return carry

    lax.fori_loop(0, 4, finish, 0)

    def done1(i, carry):
        device, src = copy1(i)

        @pl.when(not_me(device))
        def _():
            pltpu.make_async_remote_copy(
                src_ref=src, dst_ref=tok.at[frame], send_sem=s1.at[i], recv_sem=r1.at[frame],
                device_id=device, device_id_type=MESH,
            ).wait_send()

        return carry

    def done2(f, carry):
        device = target2(f)

        @pl.when(not_me(device))
        def _():
            pltpu.make_async_remote_copy(
                src_ref=mixed.at[f], dst_ref=tok2.at[f], send_sem=s2.at[f], recv_sem=r2.at[f],
                device_id=device, device_id_type=MESH,
            ).wait_send()

        return carry

    def done3(xs, carry):
        exchange(xs).wait_send()
        return carry

    def done4(g, carry):
        device = target4(g)

        @pl.when(not_me(device))
        def _():
            pltpu.make_async_remote_copy(
                src_ref=att.at[g], dst_ref=home.at[0], send_sem=s4.at[g], recv_sem=r4.at[0],
                device_id=device, device_id_type=MESH,
            ).wait_send()

        return carry

    lax.fori_loop(0, 32, done1, 0)
    lax.fori_loop(0, 32, done2, 0)
    lax.fori_loop(0, 4, done3, 0)
    lax.fori_loop(0, 8, done4, 0)


def body(
    clip, norm_time, w_time_qkv, q_gain_time, k_gain_time, w_time_out,
    norm_space, w_space_qkv, q_gain_space, k_gain_space,
):
    anywhere = pl.BlockSpec(memory_space=pl.ANY)
    vmem = pl.BlockSpec(memory_space=pltpu.VMEM)
    dma = pltpu.SemaphoreType.DMA
    flat = lambda gain: gain.reshape(1, -1)
    return pl.pallas_call(
        kernel,
        out_shape=jax.ShapeDtypeStruct((4, 1, 128, INNER), BF),
        in_specs=[anywhere, vmem, anywhere, vmem, vmem, anywhere, vmem, anywhere, vmem, vmem],
        out_specs=vmem,
        scratch_shapes=[
            pltpu.VMEM((D, 3 * INNER), BF),
            pltpu.VMEM((INNER, D), BF),
            pltpu.VMEM((D, 3 * INNER), BF),
            pltpu.VMEM((INNER, INNER), BF),
            pltpu.VMEM((128, 128), BF),
            pltpu.VMEM((128, 128), BF),
            pltpu.VMEM((32, 16, D), BF),
            pltpu.VMEM((16, 32, INNER), F32),
            pltpu.VMEM((16, 32, INNER), F32),
            pltpu.VMEM((16, 32, INNER), F32),
            pltpu.VMEM((512, INNER), BF),
            pltpu.VMEM((32, 16, D), BF),
            pltpu.VMEM((32, 16, D), BF),
            pltpu.VMEM((4, 3, 8, 16, HALF), BF),
            pltpu.VMEM((2, 4, 3, 8, 16, HALF), BF),
            pltpu.VMEM((4, 1024, 256), BF),
            pltpu.VMEM((8, 20, 16, 128), BF),
            pltpu.VMEM((8, 20, 16, 128), BF),
            dma((3,)),
            dma((32,)), dma((32,)),
            dma((32,)), dma((32,)),
            dma((4,)), dma((4,)),
            dma((8,)), dma((8,)),
        ],
        compiler_params=pltpu.CompilerParams(
            collective_id=0, has_side_effects=True, vmem_limit_bytes=58 * 2**20
        ),
        cost_estimate=pl.CostEstimate(
            flops=2 * 512 * D * (6 * INNER + INNER), bytes_accessed=14 * 2**20, transcendentals=6 * 2**20
        ),
    )(
        clip, flat(norm_time), w_time_qkv, flat(q_gain_time), flat(k_gain_time), w_time_out,
        flat(norm_space), w_space_qkv, flat(q_gain_space), flat(k_gain_space),
    )


def solution(mesh):
    in_specs = (P(None, "frame", "patch", None),) + (P(),) * 9
    out_specs = P(None, "frame", "patch", None)
    return jax.shard_map(body, mesh=mesh, in_specs=in_specs, out_specs=out_specs, check_vma=False)
```

```python
import math

import jax
import jax.numpy as jnp
from jax import lax
from jax.experimental import pallas as pl
from jax.experimental.pallas import tpu as pltpu
from jax.sharding import PartitionSpec as P

MESH = pl.DeviceIdType.MESH
HDIM = 80
HEADS = 8
D = 1280
INNER = 640
HALF = 384
EPS = 1e-06
SCALE = HDIM ** (-0.5) * math.log2(math.e)
BF = jnp.bfloat16
F32 = jnp.float32
WINDOWS = (0, 0, 128, 128, 256, 256, 384, 384)


def div(a, b):
    return lax.div(a, jnp.int32(b))


def rem(a, b):
    return lax.rem(a, jnp.int32(b))


def kernel(
    clip, norm_t, w_tqkv, qg_t, kg_t, w_out, norm_s, w_sqkv, qg_s, kg_s,
    home,
    wt, wo, ws, blocks, pmask, swap, tok, tq, tk, tv, tatt, mixed, tok2, send_qkv, qkv, vm, att,
    wsem, s1, r1, s2, r2, sq, rq, s4, r4,
):
    frame, patch = lax.axis_index("frame"), lax.axis_index("patch")
    x, zl, core = div(frame, 8), rem(div(frame, 2), 4), rem(frame, 2)
    zh, y = div(patch, 4), rem(patch, 4)
    z = zh * 4 + zl
    c, zb = div(z, 2), rem(z, 2)

    def flip(zz, cc):
        return rem(zz + 1 + rem(div(cc + 1, 2), 2), 2)

    zh_src = flip(zb, c)
    pg_src = zh_src * 4 + y

    def is_me(device):
        return (device[0] == frame) & (device[1] == patch)

    def not_me(device):
        return (device[0] != frame) | (device[1] != patch)

    def target1(i):
        xt = rem(x + zl + 4 - div(i, 8), 4)
        ct = rem(c + 1 + i, 4)
        kt = rem(div(i, 4), 2)
        zt = 2 * ct + flip(zh, ct)
        return (xt * 8 + rem(zt, 4) * 2 + kt, div(zt, 4) * 4 + y), ct, kt * 4 + xt

    def source1(i):
        return (i, pg_src)

    def target2(f):
        zt = 2 * c + rem(f, 2)
        yt = rem(div(f, 2) + c + 2 * rem(f, 2), 4)
        return (div(f, 8) * 8 + rem(zt, 4) * 2 + core, div(zt, 4) * 4 + yt)

    def source2(i):
        zs = 2 * c + rem(i, 2)
        return (div(i, 8) * 8 + rem(zs, 4) * 2 + core, div(zs, 4) * 4 + rem(div(i, 2), 4))

    home_zl = rem(y + 8 - c - 2 * zb, 4)
    home_frame = x * 8 + home_zl * 2 + zb

    def target4(g):
        return (home_frame, g)

    def source4(i):
        zs = 2 * div(i, 2) + core
        return (x * 8 + rem(zs, 4) * 2 + rem(i, 2), div(zs, 4) * 4 + rem(zl + div(i, 2) + 2 * core, 4))

    partner = (x * 8 + zl * 2 + 1 - core, patch)

    loads = (
        pltpu.make_async_copy(w_tqkv, wt, wsem.at[0]),
        pltpu.make_async_copy(w_out, wo, wsem.at[1]),
        pltpu.make_async_copy(w_sqkv, ws, wsem.at[2]),
    )
    loads[0].start()
    loads[1].start()
    loads[2].start()

    barrier = pltpu.get_barrier_semaphore()

    def greet(device):
        @pl.when(not_me(device))
        def _():
            pl.semaphore_signal(barrier, inc=1, device_id=device, device_id_type=MESH)

    def greet1(i, carry):
        greet(source1(rem(frame + i, 32)))
        return carry

    def greet2(i, carry):
        greet(source2(i))
        return carry

    def greet4(i, carry):
        greet(source4(i))
        return carry

    lax.fori_loop(0, 32, greet1, 0)
    lax.fori_loop(0, 32, greet2, 0)
    lax.fori_loop(0, 8, greet4, 0)
    greet(partner)

    rows = lax.broadcasted_iota(jnp.int32, (INNER, INNER), 0)
    cols = lax.broadcasted_iota(jnp.int32, (INNER, INNER), 1)
    head_of = lambda v: lax.shift_right_logical(v * 52429, 22)
    blocks[...] = jnp.where(head_of(rows) == head_of(cols), 1.0, 0.0).astype(BF)
    rows = lax.broadcasted_iota(jnp.int32, (128, 128), 0)
    cols = lax.broadcasted_iota(jnp.int32, (128, 128), 1)
    pmask[...] = jnp.where((rows >> 5) == (cols >> 5), 1.0, 0.0).astype(BF)
    swap[...] = jnp.where(cols == (rows & 7) * 16 + (rows >> 3), 1.0, 0.0).astype(BF)

    own1 = jnp.where(zh_src == zh, 1, 0)
    own4 = jnp.where(home_frame == frame, 1, 0)
    pl.semaphore_wait(barrier, 32 - own1 + 31 + 8 - own4 + 1)

    def copy1(i):
        device, ct, b = target1(i)
        src = clip.at[ct, 0, pl.ds(pl.multiple_of(b * 16, 16), 16)]
        return device, src

    def send1(i, carry):
        device, src = copy1(i)

        @pl.when(not_me(device))
        def _():
            pltpu.make_async_remote_copy(
                src_ref=src, dst_ref=tok.at[frame], send_sem=s1.at[i], recv_sem=r1.at[frame],
                device_id=device, device_id_type=MESH,
            ).start()

        @pl.when(is_me(device))
        def _():
            pltpu.make_async_copy(src, tok.at[frame], r1.at[frame]).start()

        return carry

    lax.fori_loop(0, 16, send1, 0)

    def layer_norm(values, gain):
        average = jnp.mean(values, axis=-1, keepdims=True)
        centred = values - average
        variance = jnp.mean(centred * centred, axis=-1, keepdims=True)
        return (centred * lax.rsqrt(variance + EPS) * gain).astype(BF)

    def head_norm(part, gain):
        squares = jnp.dot((part * part).astype(BF), blocks[...], preferred_element_type=F32)
        return (part * lax.rsqrt(squares * (1.0 / HDIM) + EPS) * gain).astype(BF)

    def project(values, norm, weight, q_gain, k_gain):
        normed = layer_norm(values, norm[...].reshape(1, -1))
        product = jnp.dot(normed, weight[...], preferred_element_type=F32)
        query = head_norm(product[:, :INNER], q_gain[...].reshape(1, -1))
        keys = head_norm(product[:, INNER : 2 * INNER], k_gain[...].reshape(1, -1))
        return query, keys, product[:, 2 * INNER :].astype(BF)

    def wait_local(src, dst, sem):
        pltpu.make_async_copy(src, dst, sem).wait()

    loads[0].wait()

    def sent1(i, carry):
        device, src = copy1(i)

        @pl.when(not_me(device))
        def _():
            pltpu.make_async_remote_copy(
                src_ref=src, dst_ref=tok.at[frame], send_sem=s1.at[i], recv_sem=r1.at[frame],
                device_id=device, device_id_type=MESH,
            ).wait_send()

        return carry

    def pairs_of(d):
        return [a * 8 + rem(d + 4 - a, 4) * 2 for a in range(4)]

    def time_project(j, carry):
        @pl.when(j < 2)
        def _():
            lax.fori_loop(0, 8, lambda i, inner: sent1(8 * j + i, inner), 0)
            lax.fori_loop(0, 8, lambda i, inner: send1(8 * j + 16 + i, inner), 0)

        d = rem(x + j, 4)
        first = pairs_of(d)
        for a in range(4):
            for k in range(2):
                slot = first[a] + k
                wait_local(tok.at[slot], tok.at[slot], r1.at[slot])
        values = jnp.concatenate([tok[pl.ds(f, 2)].reshape(32, D) for f in first], axis=0)
        values = jnp.dot(swap[...], values, preferred_element_type=F32)
        parts = project(values, norm_t, wt, qg_t, kg_t)
        at = pl.ds(pl.multiple_of(d * 8, 8), 8)
        for ref, part in zip((tq, tk, tv), parts):
            ref[:, at, :] = part.astype(F32).reshape(16, 8, INNER)
        return carry

    lax.fori_loop(0, 4, time_project, 0)
    loads[1].wait()

    lane = lax.broadcasted_iota(jnp.int32, (1, 256), 1)

    def time_attend(g, carry):
        at = pl.ds(4 * g, 4)
        tiles = [jnp.zeros((128, 128), F32)] * 5
        for h in range(HEADS):
            w = WINDOWS[h]
            first = h * HDIM - w
            mask = (lane >= first) & (lane < first + HDIM)
            spare = 255 if first + HDIM <= 255 else 0
            query = jnp.where(mask, tq[at, :, w : w + 256].reshape(128, 256), 0.0).astype(BF)
            keys = tk[at, :, w : w + 256].reshape(128, 256).astype(BF)
            scores = lax.dot_general(
                query, keys, (((1,), (1,)), ((), ())), preferred_element_type=F32
            )
            prob = jnp.exp2(scores * SCALE).astype(BF) * pmask[...]
            vals = jnp.where(mask, tv[at, :, w : w + 256].reshape(128, 256), 1.0).astype(BF)
            summed = jnp.dot(prob, vals, preferred_element_type=F32)
            result = summed * (1.0 / summed[:, spare : spare + 1])
            t = w // 128
            tiles[t] = jnp.where(mask[:, :128], result[:, :128], tiles[t])
            tiles[t + 1] = jnp.where(mask[:, 128:], result[:, 128:], tiles[t + 1])
        rows = pl.ds(pl.multiple_of(g * 128, 128), 128)
        for n in range(5):
            tatt[rows, n * 128 : (n + 1) * 128] = tiles[n].astype(BF)
        return carry

    lax.fori_loop(0, 4, time_attend, 0)

    def time_mix(j, carry):
        d = rem(x + j, 4)
        first = pairs_of(d)
        rows = lax.broadcasted_iota(jnp.int32, (128, 512), 0)
        cols = lax.broadcasted_iota(jnp.int32, (128, 512), 1)
        pick = jnp.where(cols == (rows & 15) * 32 + (rows >> 4) + d * 8, 1.0, 0.0).astype(BF)
        attended = jnp.dot(pick, tatt[...], preferred_element_type=F32).astype(BF)
        delta = jnp.dot(attended, wo[...], preferred_element_type=F32)
        for a in range(4):
            values = tok[pl.ds(first[a], 2)].reshape(32, D).astype(F32)
            total = (values + delta[32 * a : 32 * a + 32]).astype(BF)
            mixed[pl.ds(first[a], 2)] = total.reshape(2, 16, D)

        def send(i, inner):
            a = rem(x + 1 + i, 4)
            f = a * 8 + rem(x + j + 4 - a, 4) * 2 + div(i, 4)
            device = target2(f)
            slot = x * 8 + pg_src

            @pl.when(not_me(device))
            def _():
                pltpu.make_async_remote_copy(
                    src_ref=mixed.at[f], dst_ref=tok2.at[slot], send_sem=s2.at[f],
                    recv_sem=r2.at[slot], device_id=device, device_id_type=MESH,
                ).start()

            @pl.when(is_me(device))
            def _():
                pltpu.make_async_copy(mixed.at[f], tok2.at[slot], r2.at[slot]).start()

            return inner

        lax.fori_loop(0, 8, send, 0)
        return carry

    lax.fori_loop(0, 4, time_mix, 0)
    loads[2].wait()

    def exchange(xs):
        return pltpu.make_async_remote_copy(
            src_ref=send_qkv.at[xs], dst_ref=qkv.at[core, xs], send_sem=sq.at[xs],
            recv_sem=rq.at[xs], device_id=partner, device_id_type=MESH,
        )

    def space_project(j, carry):
        xs = rem(x + home_zl + 4 - j, 4)

        def wait(i, inner):
            slot = xs * 8 + i
            wait_local(tok2.at[slot], tok2.at[slot], r2.at[slot])
            return inner

        lax.fori_loop(0, 8, wait, 0)
        values = tok2[pl.ds(xs * 8, 8)].reshape(128, D).astype(F32)
        parts = project(values, norm_s, ws, qg_s, kg_s)
        for n in range(3):
            low, high = parts[n][:, :HALF], parts[n][:, INNER - HALF :]
            qkv[core, xs, n] = jnp.where(core == 0, low, high).reshape(8, 16, HALF)
            send_qkv[xs, n] = jnp.where(core == 0, high, low).reshape(8, 16, HALF)
        exchange(xs).start()
        return carry

    lax.fori_loop(0, 4, space_project, 0)

    def wait_partner(xs, carry):
        wait_local(send_qkv.at[xs], qkv.at[1 - core, xs], rq.at[xs])
        return carry

    lax.fori_loop(0, 4, wait_partner, 0)

    def head_mask(j):
        first = j * HDIM + 64 * core - (0 if j < 2 else 128)
        return (lane >= first) & (lane < first + HDIM)

    for j in range(4):
        w = 0 if j < 2 else 128
        vals = qkv[:, :, 2, :, :, w : w + 256].reshape(1024, 256)
        vm[j] = jnp.where(head_mask(j), vals, 1.0).astype(BF)

    def send4(g):
        device = target4(g)
        slot = c * 2 + core
        src, dst = att.at[g], home.at[slot]

        @pl.when(not_me(device))
        def _():
            pltpu.make_async_remote_copy(
                src_ref=src, dst_ref=dst, send_sem=s4.at[g], recv_sem=r4.at[slot],
                device_id=device, device_id_type=MESH,
            ).start()

        @pl.when(is_me(device))
        def _():
            pltpu.make_async_copy(src, dst, r4.at[slot]).start()

    def space_attend(j, carry):
        t = rem(zl + j, 4)
        tiles = [jnp.zeros((256, 128), F32)] * 3
        for h in range(4):
            w = 0 if h < 2 else 128
            spare = 255 if h < 2 else 0
            mask = head_mask(h)
            query = qkv[:, :, 0, pl.ds(2 * t, 2), :, w : w + 256].reshape(256, 256)
            query = jnp.where(mask, query, 0.0).astype(BF)
            keys = qkv[:, :, 1, :, :, w : w + 256].reshape(1024, 256)
            scores = lax.dot_general(
                query, keys, (((1,), (1,)), ((), ())), preferred_element_type=F32
            )
            prob = jnp.exp2(scores * SCALE).astype(BF)
            summed = jnp.dot(prob, vm[h], preferred_element_type=F32)
            result = summed * (1.0 / summed[:, spare : spare + 1])
            n = w // 128
            tiles[n] = jnp.where(mask[:, :128], result[:, :128], tiles[n])
            tiles[n + 1] = jnp.where(mask[:, 128:], result[:, 128:], tiles[n + 1])
        first = core == 0
        whole = [jnp.where(first, tiles[n], tiles[n + 1]).astype(BF) for n in range(2)]
        shared = jnp.where(first, tiles[2], tiles[0])
        packed = shared[:128] + pltpu.roll(shared[128:], 64, 1)
        packed = packed.astype(BF).reshape(4, 2, 16, 128)
        for g in range(2):
            for n in range(2):
                att[2 * t + g, 8 * n : 8 * n + 8] = whole[n].reshape(8, 2, 16, 128)[:, g]
            att[2 * t + g, 16:] = packed[:, g]
        send4(2 * t)
        send4(2 * t + 1)
        return carry

    lax.fori_loop(0, 4, space_attend, 0)

    def arrived(i, carry):
        wait_local(home.at[i], home.at[i], r4.at[i])
        return carry

    lax.fori_loop(0, 8, arrived, 0)

    def done2(f, carry):
        device = target2(f)

        @pl.when(not_me(device))
        def _():
            pltpu.make_async_remote_copy(
                src_ref=mixed.at[f], dst_ref=tok2.at[f], send_sem=s2.at[f], recv_sem=r2.at[f],
                device_id=device, device_id_type=MESH,
            ).wait_send()

        return carry

    def done3(xs, carry):
        exchange(xs).wait_send()
        return carry

    def done4(g, carry):
        device = target4(g)

        @pl.when(not_me(device))
        def _():
            pltpu.make_async_remote_copy(
                src_ref=att.at[g], dst_ref=home.at[0], send_sem=s4.at[g], recv_sem=r4.at[0],
                device_id=device, device_id_type=MESH,
            ).wait_send()

        return carry

    lax.fori_loop(16, 32, sent1, 0)
    lax.fori_loop(0, 32, done2, 0)
    lax.fori_loop(0, 4, done3, 0)
    lax.fori_loop(0, 8, done4, 0)


def assemble(home, out):
    for half in range(2):
        for n in range(2):
            at = (3 * half + n) * 128
            out[0, 0, :, at : at + 128] = home[half, 8 * n : 8 * n + 8].reshape(128, 128)
    low = home[0, 16:].reshape(64, 128).astype(F32)
    high = home[1, 16:].reshape(64, 128).astype(F32)
    left = lax.broadcasted_iota(jnp.int32, (1, 128), 1) < 64
    out[0, 0, :64, 256:384] = jnp.where(left, low, high).astype(BF)
    out[0, 0, 64:, 256:384] = pltpu.roll(jnp.where(left, high, low), 64, 1).astype(BF)


def body(
    clip, norm_time, w_time_qkv, q_gain_time, k_gain_time, w_time_out,
    norm_space, w_space_qkv, q_gain_space, k_gain_space,
):
    anywhere = pl.BlockSpec(memory_space=pl.ANY)
    vmem = pl.BlockSpec(memory_space=pltpu.VMEM)
    dma = pltpu.SemaphoreType.DMA
    home = pl.pallas_call(
        kernel,
        out_shape=jax.ShapeDtypeStruct((8, 20, 16, 128), BF),
        in_specs=[anywhere, vmem, anywhere, vmem, vmem, anywhere, vmem, anywhere, vmem, vmem],
        out_specs=anywhere,
        scratch_shapes=[
            pltpu.VMEM((D, 3 * INNER), BF),
            pltpu.VMEM((INNER, D), BF),
            pltpu.VMEM((D, 3 * INNER), BF),
            pltpu.VMEM((INNER, INNER), BF),
            pltpu.VMEM((128, 128), BF),
            pltpu.VMEM((128, 128), BF),
            pltpu.VMEM((32, 16, D), BF),
            pltpu.VMEM((16, 32, INNER), F32),
            pltpu.VMEM((16, 32, INNER), F32),
            pltpu.VMEM((16, 32, INNER), F32),
            pltpu.VMEM((512, INNER), BF),
            pltpu.VMEM((32, 16, D), BF),
            pltpu.VMEM((32, 16, D), BF),
            pltpu.VMEM((4, 3, 8, 16, HALF), BF),
            pltpu.VMEM((2, 4, 3, 8, 16, HALF), BF),
            pltpu.VMEM((4, 1024, 256), BF),
            pltpu.VMEM((8, 20, 16, 128), BF),
            dma((3,)),
            dma((32,)), dma((32,)),
            dma((32,)), dma((32,)),
            dma((4,)), dma((4,)),
            dma((8,)), dma((8,)),
        ],
        compiler_params=pltpu.CompilerParams(
            collective_id=0, has_side_effects=True, vmem_limit_bytes=58 * 2**20
        ),
        cost_estimate=pl.CostEstimate(
            flops=2 * 512 * D * (6 * INNER + INNER), bytes_accessed=14 * 2**20, transcendentals=6 * 2**20
        ),
    )(
        clip, norm_time, w_time_qkv, q_gain_time, k_gain_time, w_time_out,
        norm_space, w_space_qkv, q_gain_space, k_gain_space,
    )
    return pl.pallas_call(
        assemble,
        grid=(4,),
        out_shape=jax.ShapeDtypeStruct((4, 1, 128, INNER), BF),
        in_specs=[pl.BlockSpec((2, 20, 16, 128), lambda i: (i, 0, 0, 0))],
        out_specs=pl.BlockSpec((1, 1, 128, INNER), lambda i: (i, 0, 0, 0)),
    )(home)


def solution(mesh):
    in_specs = (P(None, "frame", "patch", None),) + (P(),) * 9
    out_specs = P(None, "frame", "patch", None)
    return jax.shard_map(body, mesh=mesh, in_specs=in_specs, out_specs=out_specs, check_vma=False)
```

```python
import math

import jax
import jax.numpy as jnp
from jax import lax
from jax.experimental import pallas as pl
from jax.experimental.pallas import tpu as pltpu
from jax.sharding import PartitionSpec as P

MESH = pl.DeviceIdType.MESH
HDIM = 80
HEADS = 8
D = 1280
INNER = 640
HALF = 384
EPS = 1e-06
SCALE = HDIM ** (-0.5) * math.log2(math.e)
BF = jnp.bfloat16
F32 = jnp.float32
WINDOWS = (0, 0, 128, 128, 256, 256, 384, 384)


def div(a, b):
    return lax.div(a, jnp.int32(b))


def rem(a, b):
    return lax.rem(a, jnp.int32(b))


def kernel(
    clip, norm_t, w_tqkv, qg_t, kg_t, w_out, norm_s, w_sqkv, qg_s, kg_s,
    home,
    wt, wo, ws, blocks, pmask, swap, tok, tq, tkv, tatt, mixed, tok2, send_qkv, qkv, vm, att,
    wsem, s1, r1, st, rt, s2, r2, sq, rq, s4, r4,
):
    frame, patch = lax.axis_index("frame"), lax.axis_index("patch")
    x, zl, core = div(frame, 8), rem(div(frame, 2), 4), rem(frame, 2)
    zh, y = div(patch, 4), rem(patch, 4)
    z = zh * 4 + zl
    c, zb = div(z, 2), rem(z, 2)

    def flip(zz, cc):
        return rem(zz + 1 + rem(div(cc + 1, 2), 2), 2)

    zh_src = flip(zb, c)
    pg_src = zh_src * 4 + y

    def is_me(device):
        return (device[0] == frame) & (device[1] == patch)

    def not_me(device):
        return (device[0] != frame) | (device[1] != patch)

    def target1(i):
        xt = rem(x + zl + 4 - div(rem(i, 16), 4), 4)
        ct = rem(c + 1 + i, 4)
        zt = 2 * ct + flip(zh, ct)
        device = (xt * 8 + rem(zt, 4) * 2 + core, div(zt, 4) * 4 + y)
        return device, ct, div(i, 16) * 4 + xt

    def source1(i):
        return (i * 2 + core, pg_src)

    def target2(m):
        zt = 2 * c + core
        yt = rem(rem(m, 4) + c + 2 * core, 4)
        return (div(m, 4) * 8 + rem(zt, 4) * 2 + rem(x, 2), div(zt, 4) * 4 + yt)

    def source2(i):
        xs, zs = 2 * div(i, 8) + core, 2 * c + rem(i, 2)
        return (xs * 8 + rem(zs, 4) * 2 + zb, div(zs, 4) * 4 + rem(div(i, 2), 4))

    home_zl = rem(y + 8 - c - 2 * zb, 4)
    home_frame = x * 8 + home_zl * 2 + zb

    def target4(g):
        return (home_frame, g)

    def source4(i):
        zs = 2 * div(i, 2) + core
        return (x * 8 + rem(zs, 4) * 2 + rem(i, 2), div(zs, 4) * 4 + rem(zl + div(i, 2) + 2 * core, 4))

    partner = (x * 8 + zl * 2 + 1 - core, patch)

    loads = (
        pltpu.make_async_copy(w_tqkv, wt, wsem.at[0]),
        pltpu.make_async_copy(w_out, wo, wsem.at[1]),
        pltpu.make_async_copy(w_sqkv, ws, wsem.at[2]),
    )
    loads[0].start()
    loads[1].start()
    loads[2].start()

    barrier = pltpu.get_barrier_semaphore()

    def greet(device):
        @pl.when(not_me(device))
        def _():
            pl.semaphore_signal(barrier, inc=1, device_id=device, device_id_type=MESH)

    def greet1(i, carry):
        greet(source1(i))
        return carry

    def greet2(i, carry):
        greet(source2(i))
        return carry

    def greet4(i, carry):
        greet(source4(i))
        return carry

    lax.fori_loop(0, 16, greet1, 0)
    lax.fori_loop(0, 16, greet2, 0)
    lax.fori_loop(0, 8, greet4, 0)
    greet(partner)

    rows = lax.broadcasted_iota(jnp.int32, (INNER, INNER), 0)
    cols = lax.broadcasted_iota(jnp.int32, (INNER, INNER), 1)
    head_of = lambda v: lax.shift_right_logical(v * 52429, 22)
    blocks[...] = jnp.where(head_of(rows) == head_of(cols), 1.0, 0.0).astype(BF)
    rows = lax.broadcasted_iota(jnp.int32, (128, 256), 0)
    cols = lax.broadcasted_iota(jnp.int32, (128, 256), 1)
    pmask[...] = jnp.where((rows >> 4) == ((cols & 127) >> 4), 1.0, 0.0).astype(BF)
    rows = lax.broadcasted_iota(jnp.int32, (256, 256), 0)
    cols = lax.broadcasted_iota(jnp.int32, (256, 256), 1)
    swap[...] = jnp.where(cols == (rows & 15) * 16 + (rows >> 4), 1.0, 0.0).astype(BF)

    own1 = jnp.where(zh_src == zh, 1, 0)
    own4 = jnp.where(home_frame == frame, 1, 0)
    own2 = jnp.where((core == zb) & (core == rem(x, 2)), 1, 0)
    pl.semaphore_wait(barrier, 16 - own1 + 16 - own2 + 8 - own4 + 1)

    def copy1(i):
        device, ct, b = target1(i)
        src = clip.at[ct, 0, pl.ds(pl.multiple_of(b * 16, 16), 16)]
        return device, src

    def send1(i, carry):
        device, src = copy1(i)
        slot = div(i, 16) * 16 + div(frame, 2)

        @pl.when(not_me(device))
        def _():
            pltpu.make_async_remote_copy(
                src_ref=src, dst_ref=tok.at[slot], send_sem=s1.at[i], recv_sem=r1.at[slot],
                device_id=device, device_id_type=MESH,
            ).start()

        @pl.when(is_me(device))
        def _():
            pltpu.make_async_copy(src, tok.at[slot], r1.at[slot]).start()

        return carry

    def sent1(i, carry):
        device, src = copy1(i)

        @pl.when(not_me(device))
        def _():
            pltpu.make_async_remote_copy(
                src_ref=src, dst_ref=tok.at[0], send_sem=s1.at[i], recv_sem=r1.at[0],
                device_id=device, device_id_type=MESH,
            ).wait_send()

        return carry

    lax.fori_loop(0, 16, send1, 0)

    def layer_norm(values, gain):
        average = jnp.mean(values, axis=-1, keepdims=True)
        centred = values - average
        variance = jnp.mean(centred * centred, axis=-1, keepdims=True)
        return (centred * lax.rsqrt(variance + EPS) * gain).astype(BF)

    def head_norm(part, gain):
        squares = jnp.dot((part * part).astype(BF), blocks[...], preferred_element_type=F32)
        return (part * lax.rsqrt(squares * (1.0 / HDIM) + EPS) * gain).astype(BF)

    def queries(normed, weight, gain):
        product = jnp.dot(normed, weight[:, :INNER], preferred_element_type=F32)
        return head_norm(product, gain[...].reshape(1, -1))

    def keys_values(normed, weight, gain):
        product = jnp.dot(normed, weight[:, INNER:], preferred_element_type=F32)
        return head_norm(product[:, :INNER], gain[...].reshape(1, -1)), product[:, INNER:].astype(BF)

    def wait_local(src, dst, sem):
        pltpu.make_async_copy(src, dst, sem).wait()

    for load in loads:
        load.wait()

    lane = lax.broadcasted_iota(jnp.int32, (1, 256), 1)

    def exchange_time(batch):
        return pltpu.make_async_remote_copy(
            src_ref=tkv.at[batch, core], dst_ref=tkv.at[batch, core], send_sem=st.at[batch],
            recv_sem=rt.at[batch], device_id=partner, device_id_type=MESH,
        )

    def time_attend(batch, g):
        rows = pl.ds(pl.multiple_of(g * 128, 128), 128)
        tiles = [jnp.zeros((128, 128), F32)] * 5
        for h in range(HEADS):
            w = WINDOWS[h]
            first = h * HDIM - w
            mask = (lane >= first) & (lane < first + HDIM)
            spare = 255 if first + HDIM <= 255 else 0
            query = jnp.where(mask, tq[rows, w : w + 256], 0.0).astype(BF)
            keys = tkv[batch, :, 0, rows, w : w + 256].reshape(256, 256)
            scores = lax.dot_general(
                query, keys, (((1,), (1,)), ((), ())), preferred_element_type=F32
            )
            prob = jnp.exp2(scores * SCALE).astype(BF) * pmask[...]
            vals = tkv[batch, :, 1, rows, w : w + 256].reshape(256, 256)
            vals = jnp.where(mask, vals, 1.0).astype(BF)
            summed = jnp.dot(prob, vals, preferred_element_type=F32)
            result = summed * (1.0 / summed[:, spare : spare + 1])
            t = w // 128
            tiles[t] = jnp.where(mask[:, :128], result[:, :128], tiles[t])
            tiles[t + 1] = jnp.where(mask[:, 128:], result[:, 128:], tiles[t + 1])
        for n in range(5):
            tatt[rows, n * 128 : (n + 1) * 128] = tiles[n].astype(BF)

    def send2(batch, m):
        f = batch * 16 + m
        device = target2(m)
        slot = batch * 16 + div(x, 2) * 8 + pg_src

        @pl.when(not_me(device))
        def _():
            pltpu.make_async_remote_copy(
                src_ref=mixed.at[f], dst_ref=tok2.at[slot], send_sem=s2.at[f],
                recv_sem=r2.at[slot], device_id=device, device_id_type=MESH,
            ).start()

        @pl.when(is_me(device))
        def _():
            pltpu.make_async_copy(mixed.at[f], tok2.at[slot], r2.at[slot]).start()

    def time_step(batch, carry):
        @pl.when(batch == 0)
        def _():
            for j in range(2):
                lax.fori_loop(8 * j, 8 * j + 8, sent1, 0)
                lax.fori_loop(8 * j + 16, 8 * j + 24, send1, 0)

        def wait(i, inner):
            slot = batch * 16 + i
            wait_local(tok.at[slot], tok.at[slot], r1.at[slot])
            return inner

        lax.fori_loop(0, 16, wait, 0)
        values = tok[pl.ds(batch * 16, 16)].reshape(256, D)
        values = jnp.dot(swap[...], values, preferred_element_type=F32)
        normed = layer_norm(values, norm_t[...].reshape(1, -1))
        for n, part in enumerate(keys_values(normed, wt, kg_t)):
            tkv[batch, core, n] = part
        exchange_time(batch).start()
        tq[...] = queries(normed, wt, qg_t)
        wait_local(tkv.at[batch, core], tkv.at[batch, 1 - core], rt.at[batch])

        def attend(g, inner):
            time_attend(batch, g)
            return inner

        lax.fori_loop(0, 2, attend, 0)

        def mix(half, inner):
            rows = pl.ds(pl.multiple_of(half * 128, 128), 128)
            attended = jnp.dot(swap[rows, :], tatt[...], preferred_element_type=F32).astype(BF)
            delta = jnp.dot(attended, wo[...], preferred_element_type=F32)
            at = pl.ds(batch * 16 + half * 8, 8)
            total = (tok[at].reshape(128, D).astype(F32) + delta).astype(BF)
            mixed[at] = total.reshape(8, 16, D)

            def send(i, deeper):
                send2(batch, half * 8 + rem(i, 2) * 4 + rem(div(i, 2) + x + y, 4))
                return deeper

            lax.fori_loop(0, 8, send, 0)
            return inner

        lax.fori_loop(0, 2, mix, 0)
        return carry

    lax.fori_loop(0, 2, time_step, 0)

    def exchange(batch, part):
        at = pl.ds(batch * 2, 2)
        which = pl.ds(0, 1) if part == 0 else pl.ds(1, 2)
        return pltpu.make_async_remote_copy(
            src_ref=send_qkv.at[at, which], dst_ref=qkv.at[core, at, which],
            send_sem=sq.at[batch, part], recv_sem=rq.at[batch, part],
            device_id=partner, device_id_type=MESH,
        )

    def space_step(batch, carry):
        def wait(i, inner):
            slot = batch * 16 + i
            wait_local(tok2.at[slot], tok2.at[slot], r2.at[slot])
            return inner

        lax.fori_loop(0, 16, wait, 0)
        values = tok2[pl.ds(batch * 16, 16)].reshape(256, D).astype(F32)
        normed = layer_norm(values, norm_s[...].reshape(1, -1))

        def keep(n, part):
            low, high = part[:, :HALF], part[:, INNER - HALF :]
            mine = jnp.where(core == 0, low, high).reshape(2, 8, 16, HALF)
            other = jnp.where(core == 0, high, low).reshape(2, 8, 16, HALF)
            for i in range(2):
                qkv[core, batch * 2 + i, n] = mine[i]
                send_qkv[batch * 2 + i, n] = other[i]

        for n, part in enumerate(keys_values(normed, ws, kg_s)):
            keep(1 + n, part)
        exchange(batch, 1).start()
        keep(0, queries(normed, ws, qg_s))
        exchange(batch, 0).start()
        return carry

    lax.fori_loop(0, 2, space_step, 0)

    def wait_partner(batch, carry):
        at = pl.ds(batch * 2, 2)
        for part, which in enumerate((pl.ds(0, 1), pl.ds(1, 2))):
            wait_local(send_qkv.at[at, which], qkv.at[1 - core, at, which], rq.at[batch, part])
        return carry

    lax.fori_loop(0, 2, wait_partner, 0)

    def head_mask(j):
        first = j * HDIM + 64 * core - (0 if j < 2 else 128)
        return (lane >= first) & (lane < first + HDIM)

    for j in range(4):
        w = 0 if j < 2 else 128
        vals = qkv[:, :, 2, :, :, w : w + 256].reshape(1024, 256)
        vm[j] = jnp.where(head_mask(j), vals, 1.0).astype(BF)

    def send4(g):
        device = target4(g)
        slot = c * 2 + core
        src, dst = att.at[g], home.at[slot]

        @pl.when(not_me(device))
        def _():
            pltpu.make_async_remote_copy(
                src_ref=src, dst_ref=dst, send_sem=s4.at[g], recv_sem=r4.at[slot],
                device_id=device, device_id_type=MESH,
            ).start()

        @pl.when(is_me(device))
        def _():
            pltpu.make_async_copy(src, dst, r4.at[slot]).start()

    def space_attend(j, carry):
        t = rem(zl + j, 4)
        tiles = [jnp.zeros((256, 128), F32)] * 3
        for h in range(4):
            w = 0 if h < 2 else 128
            spare = 255 if h < 2 else 0
            mask = head_mask(h)
            query = qkv[:, :, 0, pl.ds(2 * t, 2), :, w : w + 256].reshape(256, 256)
            query = jnp.where(mask, query, 0.0).astype(BF)
            keys = qkv[:, :, 1, :, :, w : w + 256].reshape(1024, 256)
            scores = lax.dot_general(
                query, keys, (((1,), (1,)), ((), ())), preferred_element_type=F32
            )
            prob = jnp.exp2(scores * SCALE).astype(BF)
            summed = jnp.dot(prob, vm[h], preferred_element_type=F32)
            result = summed * (1.0 / summed[:, spare : spare + 1])
            n = w // 128
            tiles[n] = jnp.where(mask[:, :128], result[:, :128], tiles[n])
            tiles[n + 1] = jnp.where(mask[:, 128:], result[:, 128:], tiles[n + 1])
        first = core == 0
        whole = [jnp.where(first, tiles[n], tiles[n + 1]).astype(BF) for n in range(2)]
        shared = jnp.where(first, tiles[2], tiles[0])
        packed = shared[:128] + pltpu.roll(shared[128:], 64, 1)
        packed = packed.astype(BF).reshape(4, 2, 16, 128)
        for g in range(2):
            for n in range(2):
                att[2 * t + g, 8 * n : 8 * n + 8] = whole[n].reshape(8, 2, 16, 128)[:, g]
            att[2 * t + g, 16:] = packed[:, g]
        send4(2 * t)
        send4(2 * t + 1)
        return carry

    lax.fori_loop(0, 4, space_attend, 0)

    def arrived(i, carry):
        wait_local(home.at[i], home.at[i], r4.at[i])
        return carry

    lax.fori_loop(0, 8, arrived, 0)

    def done2(f, carry):
        device = target2(rem(f, 16))

        @pl.when(not_me(device))
        def _():
            pltpu.make_async_remote_copy(
                src_ref=mixed.at[f], dst_ref=tok2.at[f], send_sem=s2.at[f], recv_sem=r2.at[f],
                device_id=device, device_id_type=MESH,
            ).wait_send()

        return carry

    def done3(batch, carry):
        exchange_time(batch).wait_send()
        exchange(batch, 0).wait_send()
        exchange(batch, 1).wait_send()
        return carry

    def done4(g, carry):
        device = target4(g)

        @pl.when(not_me(device))
        def _():
            pltpu.make_async_remote_copy(
                src_ref=att.at[g], dst_ref=home.at[0], send_sem=s4.at[g], recv_sem=r4.at[0],
                device_id=device, device_id_type=MESH,
            ).wait_send()

        return carry

    lax.fori_loop(16, 32, sent1, 0)
    lax.fori_loop(0, 32, done2, 0)
    lax.fori_loop(0, 2, done3, 0)
    lax.fori_loop(0, 8, done4, 0)


def assemble(home, out):
    def place(blocks, core, at):
        for n in range(4):
            row = (n // 2 * 4 + n % 2 * 2 + core) * 16
            out[i, 0, row : row + 16, at : at + 128] = blocks[n]

    left = lax.broadcasted_iota(jnp.int32, (1, 128), 1) < 64
    for i in range(4):
        for core in range(2):
            for half in range(2):
                for n in range(2):
                    place(home[2 * i + half, 8 * n + 4 * core : 8 * n + 4 * core + 4], core, (3 * half + n) * 128)
        low = home[2 * i, 16:].reshape(64, 128).astype(F32)
        high = home[2 * i + 1, 16:].reshape(64, 128).astype(F32)
        place(jnp.where(left, low, high).astype(BF).reshape(4, 16, 128), 0, 256)
        rolled = pltpu.roll(jnp.where(left, high, low), 64, 1)
        place(rolled.astype(BF).reshape(4, 16, 128), 1, 256)


def body(
    clip, norm_time, w_time_qkv, q_gain_time, k_gain_time, w_time_out,
    norm_space, w_space_qkv, q_gain_space, k_gain_space,
):
    anywhere = pl.BlockSpec(memory_space=pl.ANY)
    vmem = pl.BlockSpec(memory_space=pltpu.VMEM)
    dma = pltpu.SemaphoreType.DMA
    home = pl.pallas_call(
        kernel,
        out_shape=jax.ShapeDtypeStruct((8, 20, 16, 128), BF),
        in_specs=[anywhere, vmem, anywhere, vmem, vmem, anywhere, vmem, anywhere, vmem, vmem],
        out_specs=anywhere,
        scratch_shapes=[
            pltpu.VMEM((D, 3 * INNER), BF),
            pltpu.VMEM((INNER, D), BF),
            pltpu.VMEM((D, 3 * INNER), BF),
            pltpu.VMEM((INNER, INNER), BF),
            pltpu.VMEM((128, 256), BF),
            pltpu.VMEM((256, 256), BF),
            pltpu.VMEM((32, 16, D), BF),
            pltpu.VMEM((256, INNER), BF),
            pltpu.VMEM((2, 2, 2, 256, INNER), BF),
            pltpu.VMEM((256, INNER), BF),
            pltpu.VMEM((32, 16, D), BF),
            pltpu.VMEM((32, 16, D), BF),
            pltpu.VMEM((4, 3, 8, 16, HALF), BF),
            pltpu.VMEM((2, 4, 3, 8, 16, HALF), BF),
            pltpu.VMEM((4, 1024, 256), BF),
            pltpu.VMEM((8, 20, 16, 128), BF),
            dma((3,)),
            dma((32,)), dma((32,)),
            dma((2,)), dma((2,)),
            dma((32,)), dma((32,)),
            dma((2, 2)), dma((2, 2)),
            dma((8,)), dma((8,)),
        ],
        compiler_params=pltpu.CompilerParams(
            collective_id=0, has_side_effects=True, vmem_limit_bytes=58 * 2**20
        ),
        cost_estimate=pl.CostEstimate(
            flops=2 * 512 * D * (6 * INNER + INNER), bytes_accessed=14 * 2**20, transcendentals=6 * 2**20
        ),
    )(
        clip, norm_time, w_time_qkv, q_gain_time, k_gain_time, w_time_out,
        norm_space, w_space_qkv, q_gain_space, k_gain_space,
    )
    return pl.pallas_call(
        assemble,
        out_shape=jax.ShapeDtypeStruct((4, 1, 128, INNER), BF),
        in_specs=[vmem],
        out_specs=vmem,
    )(home)


def solution(mesh):
    in_specs = (P(None, "frame", "patch", None),) + (P(),) * 9
    out_specs = P(None, "frame", "patch", None)
    return jax.shard_map(body, mesh=mesh, in_specs=in_specs, out_specs=out_specs, check_vma=False)
```

```python
import math

import jax
import jax.numpy as jnp
from jax import lax
from jax.experimental import pallas as pl
from jax.experimental.pallas import tpu as pltpu
from jax.sharding import PartitionSpec as P

MESH = pl.DeviceIdType.MESH
HDIM = 80
HEADS = 8
D = 1280
INNER = 640
HALF = 384
EPS = 1e-06
SCALE = HDIM ** (-0.5) * math.log2(math.e)
BF = jnp.bfloat16
F32 = jnp.float32
WINDOWS = (0, 0, 128, 128, 256, 256, 384, 384)


def div(a, b):
    return lax.div(a, jnp.int32(b))


def rem(a, b):
    return lax.rem(a, jnp.int32(b))


def kernel(
    clip, norm_t, w_tqkv, qg_t, kg_t, w_out, norm_s, w_sqkv, qg_s, kg_s,
    home,
    wt, wo, ws, blocks, pmask, swap, tok, tq, tkv, tatt, mixed, tok2, send_qkv, qkv, vm, att,
    wsem, s1, r1, st, rt, s2, r2, sq, rq, s4, r4,
):
    frame, patch = lax.axis_index("frame"), lax.axis_index("patch")
    x, zl, core = div(frame, 8), rem(div(frame, 2), 4), rem(frame, 2)
    zh, y = div(patch, 4), rem(patch, 4)
    z = zh * 4 + zl
    c, zb = div(z, 2), rem(z, 2)

    def flip(zz, cc):
        return rem(zz + 1 + rem(div(cc + 1, 2), 2), 2)

    zh_src = flip(zb, c)
    pg_src = zh_src * 4 + y

    def is_me(device):
        return (device[0] == frame) & (device[1] == patch)

    def not_me(device):
        return (device[0] != frame) | (device[1] != patch)

    def target1(i):
        xt = rem(x + zl + 4 - div(rem(i, 16), 4), 4)
        ct = rem(c + 1 + i, 4)
        zt = 2 * ct + flip(zh, ct)
        device = (xt * 8 + rem(zt, 4) * 2 + core, div(zt, 4) * 4 + y)
        return device, ct, div(i, 16) * 4 + xt

    def source1(i):
        return (i * 2 + core, pg_src)

    def target2(m):
        zt = 2 * c + core
        yt = rem(rem(m, 4) + c + 2 * core, 4)
        return (div(m, 4) * 8 + rem(zt, 4) * 2 + rem(x, 2), div(zt, 4) * 4 + yt)

    def order2(i):
        xt = rem(x + 1 + 2 * div(i, 8) + rem(i, 2), 4)
        return xt * 4 + rem(div(i, 2) + x + y, 4)

    def source2(i):
        xs, zs = 2 * div(i, 8) + core, 2 * c + rem(i, 2)
        return (xs * 8 + rem(zs, 4) * 2 + zb, div(zs, 4) * 4 + rem(div(i, 2), 4))

    home_zl = rem(y + 8 - c - 2 * zb, 4)
    home_frame = x * 8 + home_zl * 2 + zb

    def target4(g):
        return (home_frame, g)

    def source4(i):
        zs = 2 * div(i, 2) + core
        return (x * 8 + rem(zs, 4) * 2 + rem(i, 2), div(zs, 4) * 4 + rem(zl + div(i, 2) + 2 * core, 4))

    partner = (x * 8 + zl * 2 + 1 - core, patch)

    loads = (
        pltpu.make_async_copy(w_tqkv, wt, wsem.at[0]),
        pltpu.make_async_copy(w_out, wo, wsem.at[1]),
        pltpu.make_async_copy(w_sqkv, ws, wsem.at[2]),
    )
    loads[0].start()
    loads[1].start()
    loads[2].start()

    barrier = pltpu.get_barrier_semaphore()

    def greet(device):
        @pl.when(not_me(device))
        def _():
            pl.semaphore_signal(barrier, inc=1, device_id=device, device_id_type=MESH)

    def greet1(i, carry):
        greet(source1(i))
        return carry

    def greet2(i, carry):
        greet(source2(i))
        return carry

    def greet4(i, carry):
        greet(source4(i))
        return carry

    lax.fori_loop(0, 16, greet1, 0)
    lax.fori_loop(0, 16, greet2, 0)
    lax.fori_loop(0, 8, greet4, 0)
    greet(partner)

    rows = lax.broadcasted_iota(jnp.int32, (INNER, INNER), 0)
    cols = lax.broadcasted_iota(jnp.int32, (INNER, INNER), 1)
    head_of = lambda v: lax.shift_right_logical(v * 52429, 22)
    blocks[...] = jnp.where(head_of(rows) == head_of(cols), 1.0, 0.0).astype(BF)
    rows = lax.broadcasted_iota(jnp.int32, (128, 256), 0)
    cols = lax.broadcasted_iota(jnp.int32, (128, 256), 1)
    pmask[...] = jnp.where(((rows >> 3) & 7) == ((cols >> 3) & 7), 1.0, 0.0).astype(BF)
    rows = lax.broadcasted_iota(jnp.int32, (128, 128), 0)
    cols = lax.broadcasted_iota(jnp.int32, (128, 128), 1)
    swap[...] = jnp.where(cols == (rows & 7) * 16 + (rows >> 3), 1.0, 0.0).astype(BF)

    own1 = jnp.where(zh_src == zh, 1, 0)
    own4 = jnp.where(home_frame == frame, 1, 0)
    own2 = jnp.where((core == zb) & (core == rem(x, 2)), 1, 0)
    pl.semaphore_wait(barrier, 16 - own1 + 16 - own2 + 8 - own4 + 1)

    def copy1(i):
        device, ct, b = target1(i)
        src = clip.at[ct, 0, pl.ds(pl.multiple_of(b * 16, 16), 16)]
        return device, src

    def send1(i, carry):
        device, src = copy1(i)
        slot = div(i, 16) * 16 + div(frame, 2)

        @pl.when(not_me(device))
        def _():
            pltpu.make_async_remote_copy(
                src_ref=src, dst_ref=tok.at[slot], send_sem=s1.at[i], recv_sem=r1.at[slot],
                device_id=device, device_id_type=MESH,
            ).start()

        @pl.when(is_me(device))
        def _():
            pltpu.make_async_copy(src, tok.at[slot], r1.at[slot]).start()

        return carry

    def sent1(i, carry):
        device, src = copy1(i)

        @pl.when(not_me(device))
        def _():
            pltpu.make_async_remote_copy(
                src_ref=src, dst_ref=tok.at[0], send_sem=s1.at[i], recv_sem=r1.at[0],
                device_id=device, device_id_type=MESH,
            ).wait_send()

        return carry

    lax.fori_loop(0, 16, send1, 0)

    def layer_norm(values, gain):
        average = jnp.mean(values, axis=-1, keepdims=True)
        centred = values - average
        variance = jnp.mean(centred * centred, axis=-1, keepdims=True)
        return (centred * lax.rsqrt(variance + EPS) * gain).astype(BF)

    def head_norm(part, gain):
        squares = jnp.dot((part * part).astype(BF), blocks[...], preferred_element_type=F32)
        return (part * lax.rsqrt(squares * (1.0 / HDIM) + EPS) * gain).astype(BF)

    def queries(normed, weight, gain):
        product = jnp.dot(normed, weight[:, :INNER], preferred_element_type=F32)
        return head_norm(product, gain[...].reshape(1, -1))

    def keys_values(normed, weight, gain):
        product = jnp.dot(normed, weight[:, INNER:], preferred_element_type=F32)
        return head_norm(product[:, :INNER], gain[...].reshape(1, -1)), product[:, INNER:].astype(BF)

    def wait_local(src, dst, sem):
        pltpu.make_async_copy(src, dst, sem).wait()

    for load in loads:
        load.wait()

    lane = lax.broadcasted_iota(jnp.int32, (1, 256), 1)

    def exchange_time(batch, j):
        return pltpu.make_async_remote_copy(
            src_ref=tkv.at[batch, core, :, j], dst_ref=tkv.at[batch, core, :, j],
            send_sem=st.at[batch, j], recv_sem=rt.at[batch, j],
            device_id=partner, device_id_type=MESH,
        )

    def time_attend(batch, g):
        rows = pl.ds(pl.multiple_of(g * 64, 64), 64)
        tiles = [jnp.zeros((128, 128), F32)] * 5
        for h in range(HEADS):
            w = WINDOWS[h]
            first = h * HDIM - w
            mask = (lane >= first) & (lane < first + HDIM)
            spare = 255 if first + HDIM <= 255 else 0
            query = jnp.where(mask, tq[:, rows, w : w + 256].reshape(128, 256), 0.0).astype(BF)
            keys = tkv[batch, :, 0, :, rows, w : w + 256].reshape(256, 256)
            scores = lax.dot_general(
                query, keys, (((1,), (1,)), ((), ())), preferred_element_type=F32
            )
            prob = jnp.exp2(scores * SCALE).astype(BF) * pmask[...]
            vals = tkv[batch, :, 1, :, rows, w : w + 256].reshape(256, 256)
            vals = jnp.where(mask, vals, 1.0).astype(BF)
            summed = jnp.dot(prob, vals, preferred_element_type=F32)
            result = summed * (1.0 / summed[:, spare : spare + 1])
            t = w // 128
            tiles[t] = jnp.where(mask[:, :128], result[:, :128], tiles[t])
            tiles[t + 1] = jnp.where(mask[:, 128:], result[:, 128:], tiles[t + 1])
        for n in range(5):
            tatt[:, rows, n * 128 : (n + 1) * 128] = tiles[n].astype(BF).reshape(2, 64, 128)

    def send2(batch, m):
        f = batch * 16 + m
        device = target2(m)
        slot = batch * 16 + div(x, 2) * 8 + pg_src

        @pl.when(not_me(device))
        def _():
            pltpu.make_async_remote_copy(
                src_ref=mixed.at[f], dst_ref=tok2.at[slot], send_sem=s2.at[f],
                recv_sem=r2.at[slot], device_id=device, device_id_type=MESH,
            ).start()

        @pl.when(is_me(device))
        def _():
            pltpu.make_async_copy(mixed.at[f], tok2.at[slot], r2.at[slot]).start()

    def time_step(batch, carry):
        @pl.when(batch == 0)
        def _():
            for j in range(2):
                lax.fori_loop(8 * j, 8 * j + 8, sent1, 0)
                lax.fori_loop(8 * j + 16, 8 * j + 24, send1, 0)

        def project(j, inner):
            slots = [
                batch * 16 + a * 4 + rem(x + 2 * j + k + 4 - a, 4) for a in range(4) for k in range(2)
            ]
            for slot in slots:
                wait_local(tok.at[slot], tok.at[slot], r1.at[slot])
            values = jnp.concatenate([tok[slot] for slot in slots], axis=0)
            values = jnp.dot(swap[...], values, preferred_element_type=F32)
            normed = layer_norm(values, norm_t[...].reshape(1, -1))
            for n, part in enumerate(keys_values(normed, wt, kg_t)):
                tkv[batch, core, n, j] = part
            exchange_time(batch, j).start()
            tq[j] = queries(normed, wt, qg_t)
            return inner

        lax.fori_loop(0, 2, project, 0)
        for j in range(2):
            wait_local(tkv.at[batch, core, :, j], tkv.at[batch, 1 - core, :, j], rt.at[batch, j])

        def attend(g, inner):
            time_attend(batch, g)
            return inner

        lax.fori_loop(0, 2, attend, 0)

        def mix(half, inner):
            near = [rem(x + 1 + 2 * half + i, 4) for i in range(2)]
            rows = lax.broadcasted_iota(jnp.int32, (128, 256), 0)
            cols = lax.broadcasted_iota(jnp.int32, (128, 256), 1)
            a = jnp.where(rows < 64, near[0], near[1])
            d = (a + (rows >> 4) + 8 - x) & 3
            source = (d >> 1) * 128 + (rows & 15) * 8 + a * 2 + (d & 1)
            pick = jnp.where(cols == source, 1.0, 0.0).astype(BF)
            attended = tatt[...].reshape(256, INNER)
            attended = jnp.dot(pick, attended, preferred_element_type=F32).astype(BF)
            delta = jnp.dot(attended, wo[...], preferred_element_type=F32)
            for i in range(2):
                at = pl.ds(batch * 16 + near[i] * 4, 4)
                total = (tok[at].reshape(64, D).astype(F32) + delta[64 * i : 64 * i + 64]).astype(BF)
                mixed[at] = total.reshape(4, 16, D)

            def send(i, deeper):
                send2(batch, order2(half * 8 + i))
                return deeper

            lax.fori_loop(0, 8, send, 0)
            return inner

        lax.fori_loop(0, 2, mix, 0)
        return carry

    lax.fori_loop(0, 2, time_step, 0)

    def exchange(n, part):
        which = pl.ds(0, 1) if part == 0 else pl.ds(1, 2)
        return pltpu.make_async_remote_copy(
            src_ref=send_qkv.at[n, which], dst_ref=qkv.at[core, n, which],
            send_sem=sq.at[n, part], recv_sem=rq.at[n, part],
            device_id=partner, device_id_type=MESH,
        )

    def space_step(j, carry):
        early = rem(x + 3 - rem(x + core + 1, 2), 4)
        quarter = div(j, 2) * 2 + rem(div(early, 2) + j, 2)

        def wait(i, inner):
            slot = quarter * 8 + i
            wait_local(tok2.at[slot], tok2.at[slot], r2.at[slot])
            return inner

        lax.fori_loop(0, 8, wait, 0)
        values = tok2[pl.ds(quarter * 8, 8)].reshape(128, D).astype(F32)
        normed = layer_norm(values, norm_s[...].reshape(1, -1))

        def keep(n, part):
            low, high = part[:, :HALF], part[:, INNER - HALF :]
            mine, other = jnp.where(core == 0, low, high), jnp.where(core == 0, high, low)
            qkv[core, quarter, n] = mine.reshape(2, 4, 16, HALF)
            send_qkv[quarter, n] = other.reshape(2, 4, 16, HALF)

        for n, part in enumerate(keys_values(normed, ws, kg_s)):
            keep(1 + n, part)
        exchange(quarter, 1).start()
        keep(0, queries(normed, ws, qg_s))
        exchange(quarter, 0).start()
        return carry

    lax.fori_loop(0, 4, space_step, 0)

    def wait_partner(n, carry):
        for part, which in enumerate((pl.ds(0, 1), pl.ds(1, 2))):
            wait_local(send_qkv.at[n, which], qkv.at[1 - core, n, which], rq.at[n, part])
        return carry

    lax.fori_loop(0, 4, wait_partner, 0)

    def head_mask(j):
        first = j * HDIM + 64 * core - (0 if j < 2 else 128)
        return (lane >= first) & (lane < first + HDIM)

    for j in range(4):
        w = 0 if j < 2 else 128
        vals = qkv[:, :, 2, :, :, :, w : w + 256].reshape(1024, 256)
        vm[j] = jnp.where(head_mask(j), vals, 1.0).astype(BF)

    def send4(g):
        device = target4(g)
        slot = c * 2 + core
        src, dst = att.at[g], home.at[slot]

        @pl.when(not_me(device))
        def _():
            pltpu.make_async_remote_copy(
                src_ref=src, dst_ref=dst, send_sem=s4.at[g], recv_sem=r4.at[slot],
                device_id=device, device_id_type=MESH,
            ).start()

        @pl.when(is_me(device))
        def _():
            pltpu.make_async_copy(src, dst, r4.at[slot]).start()

    def space_attend(j, carry):
        t = rem(y + z + j, 4)
        tiles = [jnp.zeros((256, 128), F32)] * 3
        for h in range(4):
            w = 0 if h < 2 else 128
            spare = 255 if h < 2 else 0
            mask = head_mask(h)
            query = qkv[:, :, 0, :, t, :, w : w + 256].reshape(256, 256)
            query = jnp.where(mask, query, 0.0).astype(BF)
            keys = qkv[:, :, 1, :, :, :, w : w + 256].reshape(1024, 256)
            scores = lax.dot_general(
                query, keys, (((1,), (1,)), ((), ())), preferred_element_type=F32
            )
            prob = jnp.exp2(scores * SCALE).astype(BF)
            summed = jnp.dot(prob, vm[h], preferred_element_type=F32)
            result = summed * (1.0 / summed[:, spare : spare + 1])
            n = w // 128
            tiles[n] = jnp.where(mask[:, :128], result[:, :128], tiles[n])
            tiles[n + 1] = jnp.where(mask[:, 128:], result[:, 128:], tiles[n + 1])
        first = core == 0
        whole = [jnp.where(first, tiles[n], tiles[n + 1]).astype(BF) for n in range(2)]
        shared = jnp.where(first, tiles[2], tiles[0])
        packed = shared[:128] + pltpu.roll(shared[128:], 64, 1)
        packed = packed.astype(BF).reshape(4, 2, 16, 128)
        for g in range(2):
            for n in range(2):
                att[4 * g + t, 8 * n : 8 * n + 8] = whole[n].reshape(8, 2, 16, 128)[:, g]
            att[4 * g + t, 16:] = packed[:, g]
        send4(t)
        send4(4 + t)
        return carry

    lax.fori_loop(0, 4, space_attend, 0)

    def arrived(i, carry):
        wait_local(home.at[i], home.at[i], r4.at[i])
        return carry

    lax.fori_loop(0, 8, arrived, 0)

    def done2(f, carry):
        device = target2(rem(f, 16))

        @pl.when(not_me(device))
        def _():
            pltpu.make_async_remote_copy(
                src_ref=mixed.at[f], dst_ref=tok2.at[f], send_sem=s2.at[f], recv_sem=r2.at[f],
                device_id=device, device_id_type=MESH,
            ).wait_send()

        return carry

    def done3(n, carry):
        exchange_time(div(n, 2), rem(n, 2)).wait_send()
        exchange(n, 0).wait_send()
        exchange(n, 1).wait_send()
        return carry

    def done4(g, carry):
        device = target4(g)

        @pl.when(not_me(device))
        def _():
            pltpu.make_async_remote_copy(
                src_ref=att.at[g], dst_ref=home.at[0], send_sem=s4.at[g], recv_sem=r4.at[0],
                device_id=device, device_id_type=MESH,
            ).wait_send()

        return carry

    lax.fori_loop(16, 32, sent1, 0)
    lax.fori_loop(0, 32, done2, 0)
    lax.fori_loop(0, 4, done3, 0)
    lax.fori_loop(0, 8, done4, 0)


def assemble(home_hbm, out_hbm, home, out, arrive, leave):
    def place(blocks, core, at):
        for n in range(4):
            row = (n // 2 * 4 + n % 2 * 2 + core) * 16
            out[i, 0, row : row + 16, at : at + 128] = blocks[n]

    left = lax.broadcasted_iota(jnp.int32, (1, 128), 1) < 64
    copies = [
        pltpu.make_async_copy(home_hbm.at[pl.ds(2 * i, 2)], home.at[pl.ds(2 * i, 2)], arrive.at[i])
        for i in range(4)
    ]
    results = [pltpu.make_async_copy(out.at[i], out_hbm.at[i], leave.at[i]) for i in range(4)]
    for copy in copies:
        copy.start()
    for i in range(4):
        copies[i].wait()
        for core in range(2):
            for half in range(2):
                for n in range(2):
                    place(home[2 * i + half, 8 * n + 4 * core : 8 * n + 4 * core + 4], core, (3 * half + n) * 128)
        low = home[2 * i, 16:].reshape(64, 128).astype(F32)
        high = home[2 * i + 1, 16:].reshape(64, 128).astype(F32)
        place(jnp.where(left, low, high).astype(BF).reshape(4, 16, 128), 0, 256)
        rolled = pltpu.roll(jnp.where(left, high, low), 64, 1)
        place(rolled.astype(BF).reshape(4, 16, 128), 1, 256)
        results[i].start()
    for result in results:
        result.wait()


def body(
    clip, norm_time, w_time_qkv, q_gain_time, k_gain_time, w_time_out,
    norm_space, w_space_qkv, q_gain_space, k_gain_space,
):
    anywhere = pl.BlockSpec(memory_space=pl.ANY)
    vmem = pl.BlockSpec(memory_space=pltpu.VMEM)
    dma = pltpu.SemaphoreType.DMA
    home = pl.pallas_call(
        kernel,
        out_shape=jax.ShapeDtypeStruct((8, 20, 16, 128), BF),
        in_specs=[anywhere, vmem, anywhere, vmem, vmem, anywhere, vmem, anywhere, vmem, vmem],
        out_specs=anywhere,
        scratch_shapes=[
            pltpu.VMEM((D, 3 * INNER), BF),
            pltpu.VMEM((INNER, D), BF),
            pltpu.VMEM((D, 3 * INNER), BF),
            pltpu.VMEM((INNER, INNER), BF),
            pltpu.VMEM((128, 256), BF),
            pltpu.VMEM((128, 128), BF),
            pltpu.VMEM((32, 16, D), BF),
            pltpu.VMEM((2, 128, INNER), BF),
            pltpu.VMEM((2, 2, 2, 2, 128, INNER), BF),
            pltpu.VMEM((2, 128, INNER), BF),
            pltpu.VMEM((32, 16, D), BF),
            pltpu.VMEM((32, 16, D), BF),
            pltpu.VMEM((4, 3, 2, 4, 16, HALF), BF),
            pltpu.VMEM((2, 4, 3, 2, 4, 16, HALF), BF),
            pltpu.VMEM((4, 1024, 256), BF),
            pltpu.VMEM((8, 20, 16, 128), BF),
            dma((3,)),
            dma((32,)), dma((32,)),
            dma((2, 2)), dma((2, 2)),
            dma((32,)), dma((32,)),
            dma((4, 2)), dma((4, 2)),
            dma((8,)), dma((8,)),
        ],
        compiler_params=pltpu.CompilerParams(
            collective_id=0, has_side_effects=True, vmem_limit_bytes=58 * 2**20
        ),
        cost_estimate=pl.CostEstimate(
            flops=2 * 512 * D * (6 * INNER + INNER), bytes_accessed=14 * 2**20, transcendentals=6 * 2**20
        ),
    )(
        clip, norm_time, w_time_qkv, q_gain_time, k_gain_time, w_time_out,
        norm_space, w_space_qkv, q_gain_space, k_gain_space,
    )
    return pl.pallas_call(
        assemble,
        out_shape=jax.ShapeDtypeStruct((4, 1, 128, INNER), BF),
        in_specs=[anywhere],
        out_specs=anywhere,
        scratch_shapes=[
            pltpu.VMEM((8, 20, 16, 128), BF),
            pltpu.VMEM((4, 1, 128, INNER), BF),
            dma((4,)), dma((4,)),
        ],
    )(home)


def solution(mesh):
    in_specs = (P(None, "frame", "patch", None),) + (P(),) * 9
    out_specs = P(None, "frame", "patch", None)
    return jax.shard_map(body, mesh=mesh, in_specs=in_specs, out_specs=out_specs, check_vma=False)
```

```python
import math

import jax
import jax.numpy as jnp
from jax import lax
from jax.experimental import pallas as pl
from jax.experimental.pallas import tpu as pltpu
from jax.sharding import PartitionSpec as P

MESH = pl.DeviceIdType.MESH
HDIM = 80
HEADS = 8
D = 1280
INNER = 640
HALF = 384
EPS = 1e-06
SCALE = HDIM ** (-0.5) * math.log2(math.e)
BF = jnp.bfloat16
F32 = jnp.float32
WINDOWS = (0, 0, 128, 128, 256, 256, 384, 384)


def div(a, b):
    return lax.div(a, jnp.int32(b))


def rem(a, b):
    return lax.rem(a, jnp.int32(b))


def kernel(
    clip, norm_t, w_tqkv, qg_t, kg_t, w_out, norm_s, w_sqkv, qg_s, kg_s,
    home,
    wt, wo, ws, blocks, pmask, swap, tok, tq, tkv, tatt, mixed, tok2, send_qkv, qkv, vm, att,
    wsem, s1, r1, st, rt, s2, r2, sq, rq, s4, r4,
):
    frame, patch = lax.axis_index("frame"), lax.axis_index("patch")
    x, zl, core = div(frame, 8), rem(div(frame, 2), 4), rem(frame, 2)
    zh, y = div(patch, 4), rem(patch, 4)
    z = zh * 4 + zl
    c, zb = div(z, 2), rem(z, 2)

    def flip(zz, cc):
        return rem(zz + 1 + rem(div(cc + 1, 2), 2), 2)

    zh_src = flip(zb, c)
    pg_src = zh_src * 4 + y

    def is_me(device):
        return (device[0] == frame) & (device[1] == patch)

    def not_me(device):
        return (device[0] != frame) | (device[1] != patch)

    def target1(i):
        xt = rem(x + zl + 4 - div(rem(i, 16), 4), 4)
        ct = rem(c + 1 + i, 4)
        zt = 2 * ct + flip(zh, ct)
        device = (xt * 8 + rem(zt, 4) * 2 + core, div(zt, 4) * 4 + y)
        return device, ct, div(i, 16) * 4 + xt

    def source1(i):
        return (i * 2 + core, pg_src)

    def target2(m):
        zt = 2 * c + core
        yt = rem(rem(m, 4) + c + 2 * core, 4)
        return (div(m, 4) * 8 + rem(zt, 4) * 2 + rem(x, 2), div(zt, 4) * 4 + yt)

    def order2(i):
        xt = rem(x + 1 + 2 * div(i, 8) + rem(i, 2), 4)
        return xt * 4 + rem(div(i, 2) + x + y, 4)

    def source2(i):
        xs, zs = 2 * div(i, 8) + core, 2 * c + rem(i, 2)
        return (xs * 8 + rem(zs, 4) * 2 + zb, div(zs, 4) * 4 + rem(div(i, 2), 4))

    home_zl = rem(y + 8 - c - 2 * zb, 4)
    home_frame = x * 8 + home_zl * 2 + zb

    def target4(g):
        return (home_frame, g)

    def source4(i):
        zs = 2 * div(i, 2) + core
        return (x * 8 + rem(zs, 4) * 2 + rem(i, 2), div(zs, 4) * 4 + rem(zl + div(i, 2) + 2 * core, 4))

    partner = (x * 8 + zl * 2 + 1 - core, patch)

    loads = (
        pltpu.make_async_copy(w_tqkv, wt, wsem.at[0]),
        pltpu.make_async_copy(w_out, wo, wsem.at[1]),
        pltpu.make_async_copy(w_sqkv, ws, wsem.at[2]),
    )
    loads[0].start()
    loads[1].start()
    loads[2].start()

    barrier = pltpu.get_barrier_semaphore()

    def greet(device):
        @pl.when(not_me(device))
        def _():
            pl.semaphore_signal(barrier, inc=1, device_id=device, device_id_type=MESH)

    def greet1(i, carry):
        greet(source1(i))
        return carry

    def greet2(i, carry):
        greet(source2(i))
        return carry

    def greet4(i, carry):
        greet(source4(i))
        return carry

    lax.fori_loop(0, 16, greet1, 0)
    lax.fori_loop(0, 16, greet2, 0)
    lax.fori_loop(0, 8, greet4, 0)
    greet(partner)

    own1 = jnp.where(zh_src == zh, 1, 0)
    own4 = jnp.where(home_frame == frame, 1, 0)
    own2 = jnp.where((core == zb) & (core == rem(x, 2)), 1, 0)
    pl.semaphore_wait(barrier, 16 - own1 + 16 - own2 + 8 - own4 + 1)

    def copy1(i):
        device, ct, b = target1(i)
        src = clip.at[ct, 0, pl.ds(pl.multiple_of(b * 16, 16), 16)]
        return device, src

    def send1(i, carry):
        device, src = copy1(i)
        slot = div(i, 16) * 16 + div(frame, 2)

        @pl.when(not_me(device))
        def _():
            pltpu.make_async_remote_copy(
                src_ref=src, dst_ref=tok.at[slot], send_sem=s1.at[i], recv_sem=r1.at[slot],
                device_id=device, device_id_type=MESH,
            ).start()

        @pl.when(is_me(device))
        def _():
            pltpu.make_async_copy(src, tok.at[slot], r1.at[slot]).start()

        return carry

    def sent1(i, carry):
        device, src = copy1(i)

        @pl.when(not_me(device))
        def _():
            pltpu.make_async_remote_copy(
                src_ref=src, dst_ref=tok.at[0], send_sem=s1.at[i], recv_sem=r1.at[0],
                device_id=device, device_id_type=MESH,
            ).wait_send()

        return carry

    lax.fori_loop(0, 16, send1, 0)

    rows = lax.broadcasted_iota(jnp.int32, (INNER, INNER), 0)
    cols = lax.broadcasted_iota(jnp.int32, (INNER, INNER), 1)
    head_of = lambda v: lax.shift_right_logical(v * 52429, 22)
    blocks[...] = jnp.where(head_of(rows) == head_of(cols), 1.0, 0.0).astype(BF)
    rows = lax.broadcasted_iota(jnp.int32, (128, 256), 0)
    cols = lax.broadcasted_iota(jnp.int32, (128, 256), 1)
    pmask[...] = jnp.where(((rows >> 3) & 7) == ((cols >> 3) & 7), 1.0, 0.0).astype(BF)
    rows = lax.broadcasted_iota(jnp.int32, (128, 128), 0)
    cols = lax.broadcasted_iota(jnp.int32, (128, 128), 1)
    swap[...] = jnp.where(cols == (rows & 7) * 16 + (rows >> 3), 1.0, 0.0).astype(BF)

    def layer_norm(values, gain):
        average = jnp.mean(values, axis=-1, keepdims=True)
        centred = values - average
        variance = jnp.mean(centred * centred, axis=-1, keepdims=True)
        return (centred * lax.rsqrt(variance + EPS) * gain).astype(BF)

    def head_norm(part, gain):
        squares = jnp.dot((part * part).astype(BF), blocks[...], preferred_element_type=F32)
        return (part * lax.rsqrt(squares * (1.0 / HDIM) + EPS) * gain).astype(BF)

    def queries(normed, weight, gain):
        product = jnp.dot(normed, weight[:, :INNER], preferred_element_type=F32)
        return head_norm(product, gain[...].reshape(1, -1))

    def keys_values(normed, weight, gain):
        product = jnp.dot(normed, weight[:, INNER:], preferred_element_type=F32)
        return head_norm(product[:, :INNER], gain[...].reshape(1, -1)), product[:, INNER:].astype(BF)

    def wait_local(src, dst, sem):
        pltpu.make_async_copy(src, dst, sem).wait()

    for load in loads:
        load.wait()

    lane = lax.broadcasted_iota(jnp.int32, (1, 256), 1)

    def exchange_time(batch, j):
        return pltpu.make_async_remote_copy(
            src_ref=tkv.at[batch, core, :, j], dst_ref=tkv.at[batch, core, :, j],
            send_sem=st.at[batch, j], recv_sem=rt.at[batch, j],
            device_id=partner, device_id_type=MESH,
        )

    def time_attend(batch, g):
        rows = pl.ds(pl.multiple_of(g * 64, 64), 64)
        tiles = [jnp.zeros((128, 128), F32)] * 5
        for h in range(HEADS):
            w = WINDOWS[h]
            first = h * HDIM - w
            mask = (lane >= first) & (lane < first + HDIM)
            spare = 255 if first + HDIM <= 255 else 0
            query = jnp.where(mask, tq[:, rows, w : w + 256].reshape(128, 256), 0.0).astype(BF)
            keys = tkv[batch, :, 0, :, rows, w : w + 256].reshape(256, 256)
            scores = lax.dot_general(
                query, keys, (((1,), (1,)), ((), ())), preferred_element_type=F32
            )
            prob = jnp.exp2(scores * SCALE).astype(BF) * pmask[...]
            vals = tkv[batch, :, 1, :, rows, w : w + 256].reshape(256, 256)
            vals = jnp.where(mask, vals, 1.0).astype(BF)
            summed = jnp.dot(prob, vals, preferred_element_type=F32)
            result = summed * (1.0 / summed[:, spare : spare + 1])
            t = w // 128
            tiles[t] = jnp.where(mask[:, :128], result[:, :128], tiles[t])
            tiles[t + 1] = jnp.where(mask[:, 128:], result[:, 128:], tiles[t + 1])
        for n in range(5):
            tatt[:, rows, n * 128 : (n + 1) * 128] = tiles[n].astype(BF).reshape(2, 64, 128)

    def send2(batch, m):
        f = batch * 16 + m
        device = target2(m)
        slot = batch * 16 + div(x, 2) * 8 + pg_src

        @pl.when(not_me(device))
        def _():
            pltpu.make_async_remote_copy(
                src_ref=mixed.at[f], dst_ref=tok2.at[slot], send_sem=s2.at[f],
                recv_sem=r2.at[slot], device_id=device, device_id_type=MESH,
            ).start()

        @pl.when(is_me(device))
        def _():
            pltpu.make_async_copy(mixed.at[f], tok2.at[slot], r2.at[slot]).start()

    def time_step(batch, carry):
        @pl.when(batch == 0)
        def _():
            for j in range(2):
                lax.fori_loop(8 * j, 8 * j + 8, sent1, 0)
                lax.fori_loop(8 * j + 16, 8 * j + 24, send1, 0)

        def project(j, inner):
            slots = [
                batch * 16 + a * 4 + rem(x + 2 * j + k + 4 - a, 4) for a in range(4) for k in range(2)
            ]
            for slot in slots:
                wait_local(tok.at[slot], tok.at[slot], r1.at[slot])
            values = jnp.concatenate([tok[slot] for slot in slots], axis=0)
            values = jnp.dot(swap[...], values, preferred_element_type=F32)
            normed = layer_norm(values, norm_t[...].reshape(1, -1))
            for n, part in enumerate(keys_values(normed, wt, kg_t)):
                tkv[batch, core, n, j] = part
            exchange_time(batch, j).start()
            tq[j] = queries(normed, wt, qg_t)
            return inner

        lax.fori_loop(0, 2, project, 0)
        for j in range(2):
            wait_local(tkv.at[batch, core, :, j], tkv.at[batch, 1 - core, :, j], rt.at[batch, j])

        def attend(g, inner):
            time_attend(batch, g)
            return inner

        lax.fori_loop(0, 2, attend, 0)

        def mix(half, inner):
            near = [rem(x + 1 + 2 * half + i, 4) for i in range(2)]
            rows = lax.broadcasted_iota(jnp.int32, (128, 256), 0)
            cols = lax.broadcasted_iota(jnp.int32, (128, 256), 1)
            a = jnp.where(rows < 64, near[0], near[1])
            d = (a + (rows >> 4) + 8 - x) & 3
            source = (d >> 1) * 128 + (rows & 15) * 8 + a * 2 + (d & 1)
            pick = jnp.where(cols == source, 1.0, 0.0).astype(BF)
            attended = tatt[...].reshape(256, INNER)
            attended = jnp.dot(pick, attended, preferred_element_type=F32).astype(BF)
            delta = jnp.dot(attended, wo[...], preferred_element_type=F32)
            for i in range(2):
                at = pl.ds(batch * 16 + near[i] * 4, 4)
                total = (tok[at].reshape(64, D).astype(F32) + delta[64 * i : 64 * i + 64]).astype(BF)
                mixed[at] = total.reshape(4, 16, D)

            def send(i, deeper):
                send2(batch, order2(half * 8 + i))
                return deeper

            lax.fori_loop(0, 8, send, 0)
            return inner

        lax.fori_loop(0, 2, mix, 0)
        return carry

    lax.fori_loop(0, 2, time_step, 0)

    def exchange(n, part):
        which = pl.ds(0, 1) if part == 0 else pl.ds(1, 2)
        return pltpu.make_async_remote_copy(
            src_ref=send_qkv.at[n, which], dst_ref=qkv.at[core, n, which],
            send_sem=sq.at[n, part], recv_sem=rq.at[n, part],
            device_id=partner, device_id_type=MESH,
        )

    def space_step(j, carry):
        early = rem(x + 3 - rem(x + core + 1, 2), 4)
        quarter = div(j, 2) * 2 + rem(div(early, 2) + j, 2)

        def wait(i, inner):
            slot = quarter * 8 + i
            wait_local(tok2.at[slot], tok2.at[slot], r2.at[slot])
            return inner

        lax.fori_loop(0, 8, wait, 0)
        values = tok2[pl.ds(quarter * 8, 8)].reshape(128, D).astype(F32)
        normed = layer_norm(values, norm_s[...].reshape(1, -1))

        def keep(n, part):
            low, high = part[:, :HALF], part[:, INNER - HALF :]
            mine, other = jnp.where(core == 0, low, high), jnp.where(core == 0, high, low)
            qkv[core, quarter, n] = mine.reshape(2, 4, 16, HALF)
            send_qkv[quarter, n] = other.reshape(2, 4, 16, HALF)

        for n, part in enumerate(keys_values(normed, ws, kg_s)):
            keep(1 + n, part)
        exchange(quarter, 1).start()
        keep(0, queries(normed, ws, qg_s))
        exchange(quarter, 0).start()
        return carry

    lax.fori_loop(0, 4, space_step, 0)

    def wait_partner(n, carry):
        for part, which in enumerate((pl.ds(0, 1), pl.ds(1, 2))):
            wait_local(send_qkv.at[n, which], qkv.at[1 - core, n, which], rq.at[n, part])
        return carry

    lax.fori_loop(0, 4, wait_partner, 0)

    def head_mask(j):
        first = j * HDIM + 64 * core - (0 if j < 2 else 128)
        return (lane >= first) & (lane < first + HDIM)

    for j in range(4):
        w = 0 if j < 2 else 128
        vals = qkv[:, :, 2, :, :, :, w : w + 256].reshape(1024, 256)
        vm[j] = jnp.where(head_mask(j), vals, 1.0).astype(BF)

    def send4(g):
        device = target4(g)
        slot = c * 2 + core
        src, dst = att.at[g], home.at[slot]

        @pl.when(not_me(device))
        def _():
            pltpu.make_async_remote_copy(
                src_ref=src, dst_ref=dst, send_sem=s4.at[g], recv_sem=r4.at[slot],
                device_id=device, device_id_type=MESH,
            ).start()

        @pl.when(is_me(device))
        def _():
            pltpu.make_async_copy(src, dst, r4.at[slot]).start()

    def space_attend(j, carry):
        t = rem(y + 1 + j, 4)
        tiles = [jnp.zeros((256, 128), F32)] * 3
        for h in range(4):
            w = 0 if h < 2 else 128
            spare = 255 if h < 2 else 0
            mask = head_mask(h)
            query = qkv[:, :, 0, :, t, :, w : w + 256].reshape(256, 256)
            query = jnp.where(mask, query, 0.0).astype(BF)
            keys = qkv[:, :, 1, :, :, :, w : w + 256].reshape(1024, 256)
            scores = lax.dot_general(
                query, keys, (((1,), (1,)), ((), ())), preferred_element_type=F32
            )
            prob = jnp.exp2(scores * SCALE).astype(BF)
            summed = jnp.dot(prob, vm[h], preferred_element_type=F32)
            result = summed * (1.0 / summed[:, spare : spare + 1])
            n = w // 128
            tiles[n] = jnp.where(mask[:, :128], result[:, :128], tiles[n])
            tiles[n + 1] = jnp.where(mask[:, 128:], result[:, 128:], tiles[n + 1])
        first = core == 0
        whole = [jnp.where(first, tiles[n], tiles[n + 1]).astype(BF) for n in range(2)]
        shared = jnp.where(first, tiles[2], tiles[0])
        packed = shared[:128] + pltpu.roll(shared[128:], 64, 1)
        packed = packed.astype(BF).reshape(4, 2, 16, 128)
        for g in range(2):
            for n in range(2):
                att[4 * g + t, 8 * n : 8 * n + 8] = whole[n].reshape(8, 2, 16, 128)[:, g]
            att[4 * g + t, 16:] = packed[:, g]
        send4((1 - zh) * 4 + t)
        send4(zh * 4 + t)
        return carry

    lax.fori_loop(0, 4, space_attend, 0)

    def done2(f, carry):
        device = target2(rem(f, 16))

        @pl.when(not_me(device))
        def _():
            pltpu.make_async_remote_copy(
                src_ref=mixed.at[f], dst_ref=tok2.at[f], send_sem=s2.at[f], recv_sem=r2.at[f],
                device_id=device, device_id_type=MESH,
            ).wait_send()

        return carry

    def done3(n, carry):
        exchange_time(div(n, 2), rem(n, 2)).wait_send()
        exchange(n, 0).wait_send()
        exchange(n, 1).wait_send()
        return carry

    def done4(g, carry):
        device = target4(g)

        @pl.when(not_me(device))
        def _():
            pltpu.make_async_remote_copy(
                src_ref=att.at[g], dst_ref=home.at[0], send_sem=s4.at[g], recv_sem=r4.at[0],
                device_id=device, device_id_type=MESH,
            ).wait_send()

        return carry

    lax.fori_loop(16, 32, sent1, 0)
    lax.fori_loop(0, 32, done2, 0)
    lax.fori_loop(0, 4, done3, 0)
    lax.fori_loop(0, 8, done4, 0)

    def arrived(i, carry):
        wait_local(home.at[i], home.at[i], r4.at[i])
        return carry

    lax.fori_loop(0, 8, arrived, 0)


def assemble(home_hbm, out_hbm, home, out, arrive, leave):
    def place(blocks, core, at):
        for n in range(4):
            row = (n // 2 * 4 + n % 2 * 2 + core) * 16
            out[i, 0, row : row + 16, at : at + 128] = blocks[n]

    left = lax.broadcasted_iota(jnp.int32, (1, 128), 1) < 64
    copies = [
        pltpu.make_async_copy(home_hbm.at[pl.ds(2 * i, 2)], home.at[pl.ds(2 * i, 2)], arrive.at[i])
        for i in range(4)
    ]
    results = [pltpu.make_async_copy(out.at[i], out_hbm.at[i], leave.at[i]) for i in range(4)]
    for copy in copies:
        copy.start()
    for i in range(4):
        copies[i].wait()
        for core in range(2):
            for half in range(2):
                for n in range(2):
                    place(home[2 * i + half, 8 * n + 4 * core : 8 * n + 4 * core + 4], core, (3 * half + n) * 128)
        low = home[2 * i, 16:].reshape(64, 128).astype(F32)
        high = home[2 * i + 1, 16:].reshape(64, 128).astype(F32)
        place(jnp.where(left, low, high).astype(BF).reshape(4, 16, 128), 0, 256)
        rolled = pltpu.roll(jnp.where(left, high, low), 64, 1)
        place(rolled.astype(BF).reshape(4, 16, 128), 1, 256)
        results[i].start()
    for result in results:
        result.wait()


def body(
    clip, norm_time, w_time_qkv, q_gain_time, k_gain_time, w_time_out,
    norm_space, w_space_qkv, q_gain_space, k_gain_space,
):
    anywhere = pl.BlockSpec(memory_space=pl.ANY)
    vmem = pl.BlockSpec(memory_space=pltpu.VMEM)
    dma = pltpu.SemaphoreType.DMA
    home = pl.pallas_call(
        kernel,
        out_shape=jax.ShapeDtypeStruct((8, 20, 16, 128), BF),
        in_specs=[anywhere, vmem, anywhere, vmem, vmem, anywhere, vmem, anywhere, vmem, vmem],
        out_specs=anywhere,
        scratch_shapes=[
            pltpu.VMEM((D, 3 * INNER), BF),
            pltpu.VMEM((INNER, D), BF),
            pltpu.VMEM((D, 3 * INNER), BF),
            pltpu.VMEM((INNER, INNER), BF),
            pltpu.VMEM((128, 256), BF),
            pltpu.VMEM((128, 128), BF),
            pltpu.VMEM((32, 16, D), BF),
            pltpu.VMEM((2, 128, INNER), BF),
            pltpu.VMEM((2, 2, 2, 2, 128, INNER), BF),
            pltpu.VMEM((2, 128, INNER), BF),
            pltpu.VMEM((32, 16, D), BF),
            pltpu.VMEM((32, 16, D), BF),
            pltpu.VMEM((4, 3, 2, 4, 16, HALF), BF),
            pltpu.VMEM((2, 4, 3, 2, 4, 16, HALF), BF),
            pltpu.VMEM((4, 1024, 256), BF),
            pltpu.VMEM((8, 20, 16, 128), BF),
            dma((3,)),
            dma((32,)), dma((32,)),
            dma((2, 2)), dma((2, 2)),
            dma((32,)), dma((32,)),
            dma((4, 2)), dma((4, 2)),
            dma((8,)), dma((8,)),
        ],
        compiler_params=pltpu.CompilerParams(
            collective_id=0, has_side_effects=True, vmem_limit_bytes=58 * 2**20
        ),
        cost_estimate=pl.CostEstimate(
            flops=2 * 512 * D * (6 * INNER + INNER), bytes_accessed=14 * 2**20, transcendentals=6 * 2**20
        ),
    )(
        clip, norm_time, w_time_qkv, q_gain_time, k_gain_time, w_time_out,
        norm_space, w_space_qkv, q_gain_space, k_gain_space,
    )
    return pl.pallas_call(
        assemble,
        out_shape=jax.ShapeDtypeStruct((4, 1, 128, INNER), BF),
        in_specs=[anywhere],
        out_specs=anywhere,
        scratch_shapes=[
            pltpu.VMEM((8, 20, 16, 128), BF),
            pltpu.VMEM((4, 1, 128, INNER), BF),
            dma((4,)), dma((4,)),
        ],
    )(home)


def solution(mesh):
    in_specs = (P(None, "frame", "patch", None),) + (P(),) * 9
    out_specs = P(None, "frame", "patch", None)
    return jax.shard_map(body, mesh=mesh, in_specs=in_specs, out_specs=out_specs, check_vma=False)
```

```python
import math

import jax
import jax.numpy as jnp
from jax import lax
from jax.experimental import pallas as pl
from jax.experimental.pallas import tpu as pltpu
from jax.sharding import PartitionSpec as P

MESH = pl.DeviceIdType.MESH
HDIM = 80
HEADS = 8
D = 1280
INNER = 640
HALF = 384
EPS = 1e-06
SCALE = HDIM ** (-0.5) * math.log2(math.e)
BF = jnp.bfloat16
F32 = jnp.float32
WINDOWS = (0, 0, 128, 128, 256, 256, 384, 384)


def div(a, b):
    return lax.div(a, jnp.int32(b))


def rem(a, b):
    return lax.rem(a, jnp.int32(b))


def kernel(
    clip, norm_t, w_tqkv, qg_t, kg_t, w_out, norm_s, w_sqkv, qg_s, kg_s,
    home,
    wt, wo, ws, blocks, pmask, swap, tok, tq, tkv, tatt, mixed, tok2, send_qkv, qkv, vm, att,
    wsem, s1, r1, st, rt, s2, r2, sq, rq, s4, r4,
):
    frame, patch = lax.axis_index("frame"), lax.axis_index("patch")
    x, zl, core = div(frame, 8), rem(div(frame, 2), 4), rem(frame, 2)
    zh, y = div(patch, 4), rem(patch, 4)
    z = zh * 4 + zl
    c, zb = div(z, 2), rem(z, 2)

    def flip(zz, cc):
        return rem(zz + 1 + rem(div(cc + 1, 2), 2), 2)

    zh_src = flip(zb, c)
    pg_src = zh_src * 4 + y

    def is_me(device):
        return (device[0] == frame) & (device[1] == patch)

    def not_me(device):
        return (device[0] != frame) | (device[1] != patch)

    def target1(i):
        xt = rem(x + zl + 4 - div(rem(i, 16), 4), 4)
        ct = rem(c + 1 + i, 4)
        zt = 2 * ct + flip(zh, ct)
        device = (xt * 8 + rem(zt, 4) * 2 + core, div(zt, 4) * 4 + y)
        return device, ct, div(i, 16) * 4 + xt

    def source1(i):
        return (i * 2 + core, pg_src)

    def target2(m):
        zt = 2 * c + core
        yt = rem(rem(m, 4) + c + 2 * core, 4)
        return (div(m, 4) * 8 + rem(zt, 4) * 2 + rem(x, 2), div(zt, 4) * 4 + yt)

    def order2(i):
        xt = rem(x + 1 + 2 * div(i, 8) + rem(i, 2), 4)
        return xt * 4 + rem(div(i, 2) + x + y, 4)

    def source2(i):
        xs, zs = 2 * div(i, 8) + core, 2 * c + rem(i, 2)
        return (xs * 8 + rem(zs, 4) * 2 + zb, div(zs, 4) * 4 + rem(div(i, 2), 4))

    home_zl = rem(y + 8 - c - 2 * zb, 4)
    home_frame = x * 8 + home_zl * 2 + zb

    def target4(g):
        return (home_frame, g)

    def source4(i):
        zs = 2 * div(i, 2) + core
        return (x * 8 + rem(zs, 4) * 2 + rem(i, 2), div(zs, 4) * 4 + rem(zl + div(i, 2) + 2 * core, 4))

    partner = (x * 8 + zl * 2 + 1 - core, patch)

    loads = (
        pltpu.make_async_copy(w_tqkv, wt, wsem.at[0]),
        pltpu.make_async_copy(w_out, wo, wsem.at[1]),
        pltpu.make_async_copy(w_sqkv, ws, wsem.at[2]),
    )
    loads[0].start()
    loads[1].start()
    loads[2].start()

    barrier = pltpu.get_barrier_semaphore()

    def greet(device):
        @pl.when(not_me(device))
        def _():
            pl.semaphore_signal(barrier, inc=1, device_id=device, device_id_type=MESH)

    def greet1(i, carry):
        greet(source1(i))
        return carry

    def greet2(i, carry):
        greet(source2(i))
        return carry

    def greet4(i, carry):
        greet(source4(i))
        return carry

    lax.fori_loop(0, 16, greet1, 0)
    lax.fori_loop(0, 16, greet2, 0)
    lax.fori_loop(0, 8, greet4, 0)
    greet(partner)

    own1 = jnp.where(zh_src == zh, 1, 0)
    own4 = jnp.where(home_frame == frame, 1, 0)
    own2 = jnp.where((core == zb) & (core == rem(x, 2)), 1, 0)
    pl.semaphore_wait(barrier, 16 - own1 + 16 - own2 + 8 - own4 + 1)

    def copy1(i):
        device, ct, b = target1(i)
        src = clip.at[ct, 0, pl.ds(pl.multiple_of(b * 16, 16), 16)]
        return device, src

    def send1(i, carry):
        device, src = copy1(i)
        slot = div(i, 16) * 16 + div(frame, 2)

        @pl.when(not_me(device))
        def _():
            pltpu.make_async_remote_copy(
                src_ref=src, dst_ref=tok.at[slot], send_sem=s1.at[i], recv_sem=r1.at[slot],
                device_id=device, device_id_type=MESH,
            ).start()

        @pl.when(is_me(device))
        def _():
            pltpu.make_async_copy(src, tok.at[slot], r1.at[slot]).start()

        return carry

    def sent1(i, carry):
        device, src = copy1(i)

        @pl.when(not_me(device))
        def _():
            pltpu.make_async_remote_copy(
                src_ref=src, dst_ref=tok.at[0], send_sem=s1.at[i], recv_sem=r1.at[0],
                device_id=device, device_id_type=MESH,
            ).wait_send()

        return carry

    lax.fori_loop(0, 16, send1, 0, unroll=True)

    rows = lax.broadcasted_iota(jnp.int32, (INNER, INNER), 0)
    cols = lax.broadcasted_iota(jnp.int32, (INNER, INNER), 1)
    head_of = lambda v: lax.shift_right_logical(v * 52429, 22)
    blocks[...] = jnp.where(head_of(rows) == head_of(cols), 1.0, 0.0).astype(BF)
    rows = lax.broadcasted_iota(jnp.int32, (128, 256), 0)
    cols = lax.broadcasted_iota(jnp.int32, (128, 256), 1)
    pmask[...] = jnp.where(((rows >> 3) & 7) == ((cols >> 3) & 7), 1.0, 0.0).astype(BF)
    rows = lax.broadcasted_iota(jnp.int32, (128, 128), 0)
    cols = lax.broadcasted_iota(jnp.int32, (128, 128), 1)
    swap[...] = jnp.where(cols == (rows & 7) * 16 + (rows >> 3), 1.0, 0.0).astype(BF)

    def layer_norm(values, gain):
        average = jnp.mean(values, axis=-1, keepdims=True)
        centred = values - average
        variance = jnp.mean(centred * centred, axis=-1, keepdims=True)
        return (centred * lax.rsqrt(variance + EPS) * gain).astype(BF)

    def head_norm(part, gain):
        squares = jnp.dot((part * part).astype(BF), blocks[...], preferred_element_type=F32)
        return (part * lax.rsqrt(squares * (1.0 / HDIM) + EPS) * gain).astype(BF)

    def queries(normed, weight, gain):
        product = jnp.dot(normed, weight[:, :INNER], preferred_element_type=F32)
        return head_norm(product, gain[...].reshape(1, -1))

    def keys_values(normed, weight, gain):
        product = jnp.dot(normed, weight[:, INNER:], preferred_element_type=F32)
        return head_norm(product[:, :INNER], gain[...].reshape(1, -1)), product[:, INNER:].astype(BF)

    def wait_local(src, dst, sem):
        pltpu.make_async_copy(src, dst, sem).wait()

    for load in loads:
        load.wait()

    lane = lax.broadcasted_iota(jnp.int32, (1, 256), 1)

    def exchange_time(batch, j):
        return pltpu.make_async_remote_copy(
            src_ref=tkv.at[batch, core, :, j], dst_ref=tkv.at[batch, core, :, j],
            send_sem=st.at[batch, j], recv_sem=rt.at[batch, j],
            device_id=partner, device_id_type=MESH,
        )

    def time_attend(batch, g):
        rows = pl.ds(pl.multiple_of(g * 64, 64), 64)
        tiles = [jnp.zeros((128, 128), F32)] * 5
        for h in range(HEADS):
            w = WINDOWS[h]
            first = h * HDIM - w
            mask = (lane >= first) & (lane < first + HDIM)
            spare = 255 if first + HDIM <= 255 else 0
            query = jnp.where(mask, tq[:, rows, w : w + 256].reshape(128, 256), 0.0).astype(BF)
            keys = tkv[batch, :, 0, :, rows, w : w + 256].reshape(256, 256)
            scores = lax.dot_general(
                query, keys, (((1,), (1,)), ((), ())), preferred_element_type=F32
            )
            prob = jnp.exp2(scores * SCALE).astype(BF) * pmask[...]
            vals = tkv[batch, :, 1, :, rows, w : w + 256].reshape(256, 256)
            vals = jnp.where(mask, vals, 1.0).astype(BF)
            summed = jnp.dot(prob, vals, preferred_element_type=F32)
            result = summed * (1.0 / summed[:, spare : spare + 1])
            t = w // 128
            tiles[t] = jnp.where(mask[:, :128], result[:, :128], tiles[t])
            tiles[t + 1] = jnp.where(mask[:, 128:], result[:, 128:], tiles[t + 1])
        for n in range(5):
            tatt[:, rows, n * 128 : (n + 1) * 128] = tiles[n].astype(BF).reshape(2, 64, 128)

    def send2(batch, m):
        f = batch * 16 + m
        device = target2(m)
        slot = batch * 16 + div(x, 2) * 8 + pg_src

        @pl.when(not_me(device))
        def _():
            pltpu.make_async_remote_copy(
                src_ref=mixed.at[f], dst_ref=tok2.at[slot], send_sem=s2.at[f],
                recv_sem=r2.at[slot], device_id=device, device_id_type=MESH,
            ).start()

        @pl.when(is_me(device))
        def _():
            pltpu.make_async_copy(mixed.at[f], tok2.at[slot], r2.at[slot]).start()

    def time_step(batch, carry):
        @pl.when(batch == 0)
        def _():
            for j in range(2):
                lax.fori_loop(8 * j, 8 * j + 8, sent1, 0)
                lax.fori_loop(8 * j + 16, 8 * j + 24, send1, 0)

        def project(j, inner):
            slots = [
                batch * 16 + a * 4 + rem(x + 2 * j + k + 4 - a, 4) for a in range(4) for k in range(2)
            ]
            for slot in slots:
                wait_local(tok.at[slot], tok.at[slot], r1.at[slot])
            values = jnp.concatenate([tok[slot] for slot in slots], axis=0)
            values = jnp.dot(swap[...], values, preferred_element_type=F32)
            normed = layer_norm(values, norm_t[...].reshape(1, -1))
            for n, part in enumerate(keys_values(normed, wt, kg_t)):
                tkv[batch, core, n, j] = part
            exchange_time(batch, j).start()
            tq[j] = queries(normed, wt, qg_t)
            return inner

        lax.fori_loop(0, 2, project, 0)
        for j in range(2):
            wait_local(tkv.at[batch, core, :, j], tkv.at[batch, 1 - core, :, j], rt.at[batch, j])

        def attend(g, inner):
            time_attend(batch, g)
            return inner

        lax.fori_loop(0, 2, attend, 0, unroll=True)

        def mix(half, inner):
            near = [rem(x + 1 + 2 * half + i, 4) for i in range(2)]
            rows = lax.broadcasted_iota(jnp.int32, (128, 256), 0)
            cols = lax.broadcasted_iota(jnp.int32, (128, 256), 1)
            a = jnp.where(rows < 64, near[0], near[1])
            d = (a + (rows >> 4) + 8 - x) & 3
            source = (d >> 1) * 128 + (rows & 15) * 8 + a * 2 + (d & 1)
            pick = jnp.where(cols == source, 1.0, 0.0).astype(BF)
            attended = tatt[...].reshape(256, INNER)
            attended = jnp.dot(pick, attended, preferred_element_type=F32).astype(BF)
            delta = jnp.dot(attended, wo[...], preferred_element_type=F32)
            for i in range(2):
                at = pl.ds(batch * 16 + near[i] * 4, 4)
                total = (tok[at].reshape(64, D).astype(F32) + delta[64 * i : 64 * i + 64]).astype(BF)
                mixed[at] = total.reshape(4, 16, D)

            def send(i, deeper):
                send2(batch, order2(half * 8 + i))
                return deeper

            lax.fori_loop(0, 8, send, 0, unroll=True)
            return inner

        lax.fori_loop(0, 2, mix, 0, unroll=True)
        return carry

    lax.fori_loop(0, 2, time_step, 0)

    def exchange(n, part):
        which = pl.ds(0, 1) if part == 0 else pl.ds(1, 2)
        return pltpu.make_async_remote_copy(
            src_ref=send_qkv.at[n, which], dst_ref=qkv.at[core, n, which],
            send_sem=sq.at[n, part], recv_sem=rq.at[n, part],
            device_id=partner, device_id_type=MESH,
        )

    def space_step(j, carry):
        early = rem(x + 3 - rem(x + core + 1, 2), 4)
        quarter = div(j, 2) * 2 + rem(div(early, 2) + j, 2)

        def wait(i, inner):
            slot = quarter * 8 + i
            wait_local(tok2.at[slot], tok2.at[slot], r2.at[slot])
            return inner

        lax.fori_loop(0, 8, wait, 0, unroll=True)
        values = tok2[pl.ds(quarter * 8, 8)].reshape(128, D).astype(F32)
        normed = layer_norm(values, norm_s[...].reshape(1, -1))

        def keep(n, part):
            low, high = part[:, :HALF], part[:, INNER - HALF :]
            mine, other = jnp.where(core == 0, low, high), jnp.where(core == 0, high, low)
            qkv[core, quarter, n] = mine.reshape(2, 4, 16, HALF)
            send_qkv[quarter, n] = other.reshape(2, 4, 16, HALF)

        for n, part in enumerate(keys_values(normed, ws, kg_s)):
            keep(1 + n, part)
        exchange(quarter, 1).start()
        keep(0, queries(normed, ws, qg_s))
        exchange(quarter, 0).start()
        return carry

    lax.fori_loop(0, 4, space_step, 0)

    def wait_partner(n, carry):
        for part, which in enumerate((pl.ds(0, 1), pl.ds(1, 2))):
            wait_local(send_qkv.at[n, which], qkv.at[1 - core, n, which], rq.at[n, part])
        return carry

    lax.fori_loop(0, 4, wait_partner, 0)

    def head_mask(j):
        first = j * HDIM + 64 * core - (0 if j < 2 else 128)
        return (lane >= first) & (lane < first + HDIM)

    for j in range(4):
        w = 0 if j < 2 else 128
        vals = qkv[:, :, 2, :, :, :, w : w + 256].reshape(1024, 256)
        vm[j] = jnp.where(head_mask(j), vals, 1.0).astype(BF)

    def send4(g):
        device = target4(g)
        slot = c * 2 + core
        src, dst = att.at[g], home.at[slot]

        @pl.when(not_me(device))
        def _():
            pltpu.make_async_remote_copy(
                src_ref=src, dst_ref=dst, send_sem=s4.at[g], recv_sem=r4.at[slot],
                device_id=device, device_id_type=MESH,
            ).start()

        @pl.when(is_me(device))
        def _():
            pltpu.make_async_copy(src, dst, r4.at[slot]).start()

    def space_attend(j, carry):
        t = rem(y + 1 + j, 4)
        tiles = [jnp.zeros((256, 128), F32)] * 3
        for h in range(4):
            w = 0 if h < 2 else 128
            spare = 255 if h < 2 else 0
            mask = head_mask(h)
            query = qkv[:, :, 0, :, t, :, w : w + 256].reshape(256, 256)
            query = jnp.where(mask, query, 0.0).astype(BF)
            keys = qkv[:, :, 1, :, :, :, w : w + 256].reshape(1024, 256)
            scores = lax.dot_general(
                query, keys, (((1,), (1,)), ((), ())), preferred_element_type=F32
            )
            prob = jnp.exp2(scores * SCALE).astype(BF)
            summed = jnp.dot(prob, vm[h], preferred_element_type=F32)
            result = summed * (1.0 / summed[:, spare : spare + 1])
            n = w // 128
            tiles[n] = jnp.where(mask[:, :128], result[:, :128], tiles[n])
            tiles[n + 1] = jnp.where(mask[:, 128:], result[:, 128:], tiles[n + 1])
        first = core == 0
        whole = [jnp.where(first, tiles[n], tiles[n + 1]).astype(BF) for n in range(2)]
        shared = jnp.where(first, tiles[2], tiles[0])
        packed = shared[:128] + pltpu.roll(shared[128:], 64, 1)
        packed = packed.astype(BF).reshape(4, 2, 16, 128)
        for g in range(2):
            for n in range(2):
                att[4 * g + t, 8 * n : 8 * n + 8] = whole[n].reshape(8, 2, 16, 128)[:, g]
            att[4 * g + t, 16:] = packed[:, g]
        send4((1 - zh) * 4 + t)
        send4(zh * 4 + t)
        return carry

    lax.fori_loop(0, 4, space_attend, 0)

    def done2(f, carry):
        device = target2(rem(f, 16))

        @pl.when(not_me(device))
        def _():
            pltpu.make_async_remote_copy(
                src_ref=mixed.at[f], dst_ref=tok2.at[f], send_sem=s2.at[f], recv_sem=r2.at[f],
                device_id=device, device_id_type=MESH,
            ).wait_send()

        return carry

    def done3(n, carry):
        exchange_time(div(n, 2), rem(n, 2)).wait_send()
        exchange(n, 0).wait_send()
        exchange(n, 1).wait_send()
        return carry

    def done4(g, carry):
        device = target4(g)

        @pl.when(not_me(device))
        def _():
            pltpu.make_async_remote_copy(
                src_ref=att.at[g], dst_ref=home.at[0], send_sem=s4.at[g], recv_sem=r4.at[0],
                device_id=device, device_id_type=MESH,
            ).wait_send()

        return carry

    lax.fori_loop(16, 32, sent1, 0)
    lax.fori_loop(0, 32, done2, 0)
    lax.fori_loop(0, 4, done3, 0)
    lax.fori_loop(0, 8, done4, 0)

    def arrived(i, carry):
        wait_local(home.at[i], home.at[i], r4.at[i])
        return carry

    lax.fori_loop(0, 8, arrived, 0)


def assemble(home_hbm, out_hbm, home, out, arrive, leave):
    def place(blocks, core, at):
        for n in range(4):
            row = (n // 2 * 4 + n % 2 * 2 + core) * 16
            out[i, 0, row : row + 16, at : at + 128] = blocks[n]

    left = lax.broadcasted_iota(jnp.int32, (1, 128), 1) < 64
    copies = [
        pltpu.make_async_copy(home_hbm.at[pl.ds(2 * i, 2)], home.at[pl.ds(2 * i, 2)], arrive.at[i])
        for i in range(4)
    ]
    results = [pltpu.make_async_copy(out.at[i], out_hbm.at[i], leave.at[i]) for i in range(4)]
    for copy in copies:
        copy.start()
    for i in range(4):
        copies[i].wait()
        for core in range(2):
            for half in range(2):
                for n in range(2):
                    place(home[2 * i + half, 8 * n + 4 * core : 8 * n + 4 * core + 4], core, (3 * half + n) * 128)
        low = home[2 * i, 16:].reshape(64, 128).astype(F32)
        high = home[2 * i + 1, 16:].reshape(64, 128).astype(F32)
        place(jnp.where(left, low, high).astype(BF).reshape(4, 16, 128), 0, 256)
        rolled = pltpu.roll(jnp.where(left, high, low), 64, 1)
        place(rolled.astype(BF).reshape(4, 16, 128), 1, 256)
        results[i].start()
    for result in results:
        result.wait()


def body(
    clip, norm_time, w_time_qkv, q_gain_time, k_gain_time, w_time_out,
    norm_space, w_space_qkv, q_gain_space, k_gain_space,
):
    anywhere = pl.BlockSpec(memory_space=pl.ANY)
    vmem = pl.BlockSpec(memory_space=pltpu.VMEM)
    dma = pltpu.SemaphoreType.DMA
    home = pl.pallas_call(
        kernel,
        out_shape=jax.ShapeDtypeStruct((8, 20, 16, 128), BF),
        in_specs=[anywhere, vmem, anywhere, vmem, vmem, anywhere, vmem, anywhere, vmem, vmem],
        out_specs=anywhere,
        scratch_shapes=[
            pltpu.VMEM((D, 3 * INNER), BF),
            pltpu.VMEM((INNER, D), BF),
            pltpu.VMEM((D, 3 * INNER), BF),
            pltpu.VMEM((INNER, INNER), BF),
            pltpu.VMEM((128, 256), BF),
            pltpu.VMEM((128, 128), BF),
            pltpu.VMEM((32, 16, D), BF),
            pltpu.VMEM((2, 128, INNER), BF),
            pltpu.VMEM((2, 2, 2, 2, 128, INNER), BF),
            pltpu.VMEM((2, 128, INNER), BF),
            pltpu.VMEM((32, 16, D), BF),
            pltpu.VMEM((32, 16, D), BF),
            pltpu.VMEM((4, 3, 2, 4, 16, HALF), BF),
            pltpu.VMEM((2, 4, 3, 2, 4, 16, HALF), BF),
            pltpu.VMEM((4, 1024, 256), BF),
            pltpu.VMEM((8, 20, 16, 128), BF),
            dma((3,)),
            dma((32,)), dma((32,)),
            dma((2, 2)), dma((2, 2)),
            dma((32,)), dma((32,)),
            dma((4, 2)), dma((4, 2)),
            dma((8,)), dma((8,)),
        ],
        compiler_params=pltpu.CompilerParams(
            collective_id=0, has_side_effects=True, vmem_limit_bytes=58 * 2**20
        ),
        cost_estimate=pl.CostEstimate(
            flops=2 * 512 * D * (6 * INNER + INNER), bytes_accessed=14 * 2**20, transcendentals=6 * 2**20
        ),
    )(
        clip, norm_time, w_time_qkv, q_gain_time, k_gain_time, w_time_out,
        norm_space, w_space_qkv, q_gain_space, k_gain_space,
    )
    return pl.pallas_call(
        assemble,
        out_shape=jax.ShapeDtypeStruct((4, 1, 128, INNER), BF),
        in_specs=[anywhere],
        out_specs=anywhere,
        scratch_shapes=[
            pltpu.VMEM((8, 20, 16, 128), BF),
            pltpu.VMEM((4, 1, 128, INNER), BF),
            dma((4,)), dma((4,)),
        ],
    )(home)


def solution(mesh):
    in_specs = (P(None, "frame", "patch", None),) + (P(),) * 9
    out_specs = P(None, "frame", "patch", None)
    return jax.shard_map(body, mesh=mesh, in_specs=in_specs, out_specs=out_specs, check_vma=False)
```

```python
import math

import jax
import jax.numpy as jnp
from jax import lax
from jax.experimental import pallas as pl
from jax.experimental.pallas import tpu as pltpu
from jax.sharding import PartitionSpec as P

MESH = pl.DeviceIdType.MESH
HDIM = 80
HEADS = 8
D = 1280
INNER = 640
HALF = 384
EPS = 1e-06
SCALE = HDIM ** (-0.5) * math.log2(math.e)
BF = jnp.bfloat16
F32 = jnp.float32
WINDOWS = (0, 0, 128, 128, 256, 256, 384, 384)


def div(a, b):
    return lax.div(a, jnp.int32(b))


def rem(a, b):
    return lax.rem(a, jnp.int32(b))


def kernel(
    clip, norm_t, w_tqkv, qg_t, kg_t, w_out, norm_s, w_sqkv, qg_s, kg_s,
    home,
    wt, wo, ws, blocks, pmask, swap, tok, tq, tkv, tatt, mixed, tok2, send_qkv, qkv, vm, att,
    wsem, s1, r1, st, rt, s2, r2, sq, rq, s4, r4,
):
    frame, patch = lax.axis_index("frame"), lax.axis_index("patch")
    x, zl, core = div(frame, 8), rem(div(frame, 2), 4), rem(frame, 2)
    zh, y = div(patch, 4), rem(patch, 4)
    z = zh * 4 + zl
    c, zb = div(z, 2), rem(z, 2)

    def flip(zz, cc):
        return rem(zz + 1 + rem(div(cc + 1, 2), 2), 2)

    zh_src = flip(zb, c)
    pg_src = zh_src * 4 + y

    def is_me(device):
        return (device[0] == frame) & (device[1] == patch)

    def not_me(device):
        return (device[0] != frame) | (device[1] != patch)

    def target1(i):
        xt = rem(x + zl + 4 - div(rem(i, 16), 4), 4)
        ct = rem(c + 1 + i, 4)
        zt = 2 * ct + flip(zh, ct)
        device = (xt * 8 + rem(zt, 4) * 2 + core, div(zt, 4) * 4 + y)
        return device, ct, div(i, 16) * 4 + xt

    def source1(i):
        return (i * 2 + core, pg_src)

    def target2(m):
        zt = 2 * c + core
        yt = rem(rem(m, 4) + c + 2 * core, 4)
        return (div(m, 4) * 8 + rem(zt, 4) * 2 + rem(x, 2), div(zt, 4) * 4 + yt)

    def order2(i):
        xt = rem(x + 1 + 2 * div(i, 8) + rem(i, 2), 4)
        return xt * 4 + rem(div(i, 2) + x + y, 4)

    def source2(i):
        xs, zs = 2 * div(i, 8) + core, 2 * c + rem(i, 2)
        return (xs * 8 + rem(zs, 4) * 2 + zb, div(zs, 4) * 4 + rem(div(i, 2), 4))

    home_zl = rem(y + 8 - c - 2 * zb, 4)
    home_frame = x * 8 + home_zl * 2 + zb

    def target4(g):
        return (home_frame, g)

    def source4(i):
        zs = 2 * div(i, 2) + core
        return (x * 8 + rem(zs, 4) * 2 + rem(i, 2), div(zs, 4) * 4 + rem(zl + div(i, 2) + 2 * core, 4))

    partner = (x * 8 + zl * 2 + 1 - core, patch)

    loads = (
        pltpu.make_async_copy(w_tqkv, wt, wsem.at[0]),
        pltpu.make_async_copy(w_out, wo, wsem.at[1]),
        pltpu.make_async_copy(w_sqkv, ws, wsem.at[2]),
    )
    loads[0].start()
    loads[1].start()
    loads[2].start()

    barrier = pltpu.get_barrier_semaphore()

    def greet(device):
        @pl.when(not_me(device))
        def _():
            pl.semaphore_signal(barrier, inc=1, device_id=device, device_id_type=MESH)

    def greet1(i, carry):
        greet(source1(i))
        return carry

    def greet2(i, carry):
        greet(source2(i))
        return carry

    def greet4(i, carry):
        greet(source4(i))
        return carry

    lax.fori_loop(0, 16, greet1, 0, unroll=True)
    lax.fori_loop(0, 16, greet2, 0, unroll=True)
    lax.fori_loop(0, 8, greet4, 0, unroll=True)
    greet(partner)

    own1 = jnp.where(zh_src == zh, 1, 0)
    own4 = jnp.where(home_frame == frame, 1, 0)
    own2 = jnp.where((core == zb) & (core == rem(x, 2)), 1, 0)
    pl.semaphore_wait(barrier, 16 - own1 + 16 - own2 + 8 - own4 + 1)

    def copy1(i):
        device, ct, b = target1(i)
        src = clip.at[ct, 0, pl.ds(pl.multiple_of(b * 16, 16), 16)]
        return device, src

    def send1(i, carry):
        device, src = copy1(i)
        slot = div(i, 16) * 16 + div(frame, 2)

        @pl.when(not_me(device))
        def _():
            pltpu.make_async_remote_copy(
                src_ref=src, dst_ref=tok.at[slot], send_sem=s1.at[i], recv_sem=r1.at[slot],
                device_id=device, device_id_type=MESH,
            ).start()

        @pl.when(is_me(device))
        def _():
            pltpu.make_async_copy(src, tok.at[slot], r1.at[slot]).start()

        return carry

    def sent1(i, carry):
        device, src = copy1(i)

        @pl.when(not_me(device))
        def _():
            pltpu.make_async_remote_copy(
                src_ref=src, dst_ref=tok.at[0], send_sem=s1.at[i], recv_sem=r1.at[0],
                device_id=device, device_id_type=MESH,
            ).wait_send()

        return carry

    lax.fori_loop(0, 16, send1, 0, unroll=True)

    rows = lax.broadcasted_iota(jnp.int32, (INNER, INNER), 0)
    cols = lax.broadcasted_iota(jnp.int32, (INNER, INNER), 1)
    head_of = lambda v: lax.shift_right_logical(v * 52429, 22)
    blocks[...] = jnp.where(head_of(rows) == head_of(cols), 1.0, 0.0).astype(BF)
    rows = lax.broadcasted_iota(jnp.int32, (128, 256), 0)
    cols = lax.broadcasted_iota(jnp.int32, (128, 256), 1)
    pmask[...] = jnp.where(((rows >> 3) & 7) == ((cols >> 3) & 7), 1.0, 0.0).astype(BF)
    rows = lax.broadcasted_iota(jnp.int32, (128, 128), 0)
    cols = lax.broadcasted_iota(jnp.int32, (128, 128), 1)
    swap[...] = jnp.where(cols == (rows & 7) * 16 + (rows >> 3), 1.0, 0.0).astype(BF)

    def layer_norm(values, gain):
        average = jnp.mean(values, axis=-1, keepdims=True)
        centred = values - average
        variance = jnp.mean(centred * centred, axis=-1, keepdims=True)
        return (centred * lax.rsqrt(variance + EPS) * gain).astype(BF)

    def head_norm(part, gain):
        squares = jnp.dot((part * part).astype(BF), blocks[...], preferred_element_type=F32)
        return (part * lax.rsqrt(squares * (1.0 / HDIM) + EPS) * gain).astype(BF)

    def queries(normed, weight, gain):
        product = jnp.dot(normed, weight[:, :INNER], preferred_element_type=F32)
        return head_norm(product, gain[...].reshape(1, -1))

    def keys_values(normed, weight, gain):
        product = jnp.dot(normed, weight[:, INNER:], preferred_element_type=F32)
        return head_norm(product[:, :INNER], gain[...].reshape(1, -1)), product[:, INNER:].astype(BF)

    def wait_local(src, dst, sem):
        pltpu.make_async_copy(src, dst, sem).wait()

    for load in loads:
        load.wait()

    lane = lax.broadcasted_iota(jnp.int32, (1, 256), 1)

    def exchange_time(batch, j):
        return pltpu.make_async_remote_copy(
            src_ref=tkv.at[batch, core, :, j], dst_ref=tkv.at[batch, core, :, j],
            send_sem=st.at[batch, j], recv_sem=rt.at[batch, j],
            device_id=partner, device_id_type=MESH,
        )

    def time_attend(batch, g):
        rows = pl.ds(pl.multiple_of(g * 64, 64), 64)
        tiles = [jnp.zeros((128, 128), F32)] * 5
        for h in range(HEADS):
            w = WINDOWS[h]
            first = h * HDIM - w
            mask = (lane >= first) & (lane < first + HDIM)
            spare = 255 if first + HDIM <= 255 else 0
            query = jnp.where(mask, tq[:, rows, w : w + 256].reshape(128, 256), 0.0).astype(BF)
            keys = tkv[batch, :, 0, :, rows, w : w + 256].reshape(256, 256)
            scores = lax.dot_general(
                query, keys, (((1,), (1,)), ((), ())), preferred_element_type=F32
            )
            prob = jnp.exp2(scores * SCALE).astype(BF) * pmask[...]
            vals = tkv[batch, :, 1, :, rows, w : w + 256].reshape(256, 256)
            vals = jnp.where(mask, vals, 1.0).astype(BF)
            summed = jnp.dot(prob, vals, preferred_element_type=F32)
            result = summed * (1.0 / summed[:, spare : spare + 1])
            t = w // 128
            tiles[t] = jnp.where(mask[:, :128], result[:, :128], tiles[t])
            tiles[t + 1] = jnp.where(mask[:, 128:], result[:, 128:], tiles[t + 1])
        for n in range(5):
            tatt[:, rows, n * 128 : (n + 1) * 128] = tiles[n].astype(BF).reshape(2, 64, 128)

    def send2(batch, m):
        f = batch * 16 + m
        device = target2(m)
        slot = batch * 16 + div(x, 2) * 8 + pg_src

        @pl.when(not_me(device))
        def _():
            pltpu.make_async_remote_copy(
                src_ref=mixed.at[f], dst_ref=tok2.at[slot], send_sem=s2.at[f],
                recv_sem=r2.at[slot], device_id=device, device_id_type=MESH,
            ).start()

        @pl.when(is_me(device))
        def _():
            pltpu.make_async_copy(mixed.at[f], tok2.at[slot], r2.at[slot]).start()

    def time_step(batch, carry):
        @pl.when(batch == 0)
        def _():
            for j in range(2):
                lax.fori_loop(8 * j, 8 * j + 8, sent1, 0, unroll=True)
                lax.fori_loop(8 * j + 16, 8 * j + 24, send1, 0, unroll=True)

        def project(j, inner):
            slots = [
                batch * 16 + a * 4 + rem(x + 2 * j + k + 4 - a, 4) for a in range(4) for k in range(2)
            ]
            for slot in slots:
                wait_local(tok.at[slot], tok.at[slot], r1.at[slot])
            values = jnp.concatenate([tok[slot] for slot in slots], axis=0)
            values = jnp.dot(swap[...], values, preferred_element_type=F32)
            normed = layer_norm(values, norm_t[...].reshape(1, -1))
            for n, part in enumerate(keys_values(normed, wt, kg_t)):
                tkv[batch, core, n, j] = part
            exchange_time(batch, j).start()
            tq[j] = queries(normed, wt, qg_t)
            return inner

        lax.fori_loop(0, 2, project, 0)
        for j in range(2):
            wait_local(tkv.at[batch, core, :, j], tkv.at[batch, 1 - core, :, j], rt.at[batch, j])

        def attend(g, inner):
            time_attend(batch, g)
            return inner

        lax.fori_loop(0, 2, attend, 0, unroll=True)

        def mix(half, inner):
            near = [rem(x + 1 + 2 * half + i, 4) for i in range(2)]
            rows = lax.broadcasted_iota(jnp.int32, (128, 256), 0)
            cols = lax.broadcasted_iota(jnp.int32, (128, 256), 1)
            a = jnp.where(rows < 64, near[0], near[1])
            d = (a + (rows >> 4) + 8 - x) & 3
            source = (d >> 1) * 128 + (rows & 15) * 8 + a * 2 + (d & 1)
            pick = jnp.where(cols == source, 1.0, 0.0).astype(BF)
            attended = tatt[...].reshape(256, INNER)
            attended = jnp.dot(pick, attended, preferred_element_type=F32).astype(BF)
            delta = jnp.dot(attended, wo[...], preferred_element_type=F32)
            for i in range(2):
                at = pl.ds(batch * 16 + near[i] * 4, 4)
                total = (tok[at].reshape(64, D).astype(F32) + delta[64 * i : 64 * i + 64]).astype(BF)
                mixed[at] = total.reshape(4, 16, D)

            def send(i, deeper):
                send2(batch, order2(half * 8 + i))
                return deeper

            lax.fori_loop(0, 8, send, 0, unroll=True)
            return inner

        lax.fori_loop(0, 2, mix, 0, unroll=True)
        return carry

    lax.fori_loop(0, 2, time_step, 0)

    def exchange(n, part):
        which = pl.ds(0, 1) if part == 0 else pl.ds(1, 2)
        return pltpu.make_async_remote_copy(
            src_ref=send_qkv.at[n, which], dst_ref=qkv.at[core, n, which],
            send_sem=sq.at[n, part], recv_sem=rq.at[n, part],
            device_id=partner, device_id_type=MESH,
        )

    def space_step(j, carry):
        early = rem(x + 3 - rem(x + core + 1, 2), 4)
        quarter = div(j, 2) * 2 + rem(div(early, 2) + j, 2)

        def wait(i, inner):
            slot = quarter * 8 + i
            wait_local(tok2.at[slot], tok2.at[slot], r2.at[slot])
            return inner

        lax.fori_loop(0, 8, wait, 0, unroll=True)
        values = tok2[pl.ds(quarter * 8, 8)].reshape(128, D).astype(F32)
        normed = layer_norm(values, norm_s[...].reshape(1, -1))

        def keep(n, part):
            low, high = part[:, :HALF], part[:, INNER - HALF :]
            mine, other = jnp.where(core == 0, low, high), jnp.where(core == 0, high, low)
            qkv[core, quarter, n] = mine.reshape(2, 4, 16, HALF)
            send_qkv[quarter, n] = other.reshape(2, 4, 16, HALF)

        for n, part in enumerate(keys_values(normed, ws, kg_s)):
            keep(1 + n, part)
        exchange(quarter, 1).start()
        keep(0, queries(normed, ws, qg_s))
        exchange(quarter, 0).start()
        return carry

    lax.fori_loop(0, 4, space_step, 0)

    def wait_partner(n, carry):
        for part, which in enumerate((pl.ds(0, 1), pl.ds(1, 2))):
            wait_local(send_qkv.at[n, which], qkv.at[1 - core, n, which], rq.at[n, part])
        return carry

    lax.fori_loop(0, 4, wait_partner, 0)

    def head_mask(j):
        first = j * HDIM + 64 * core - (0 if j < 2 else 128)
        return (lane >= first) & (lane < first + HDIM)

    for j in range(4):
        w = 0 if j < 2 else 128
        vals = qkv[:, :, 2, :, :, :, w : w + 256].reshape(1024, 256)
        vm[j] = jnp.where(head_mask(j), vals, 1.0).astype(BF)

    def send4(g):
        device = target4(g)
        slot = c * 2 + core
        src, dst = att.at[g], home.at[slot]

        @pl.when(not_me(device))
        def _():
            pltpu.make_async_remote_copy(
                src_ref=src, dst_ref=dst, send_sem=s4.at[g], recv_sem=r4.at[slot],
                device_id=device, device_id_type=MESH,
            ).start()

        @pl.when(is_me(device))
        def _():
            pltpu.make_async_copy(src, dst, r4.at[slot]).start()

    def space_attend(j, carry):
        t = rem(y + 1 + j, 4)
        tiles = [jnp.zeros((256, 128), F32)] * 3
        for h in range(4):
            w = 0 if h < 2 else 128
            spare = 255 if h < 2 else 0
            mask = head_mask(h)
            query = qkv[:, :, 0, :, t, :, w : w + 256].reshape(256, 256)
            query = jnp.where(mask, query, 0.0).astype(BF)
            keys = qkv[:, :, 1, :, :, :, w : w + 256].reshape(1024, 256)
            scores = lax.dot_general(
                query, keys, (((1,), (1,)), ((), ())), preferred_element_type=F32
            )
            prob = jnp.exp2(scores * SCALE).astype(BF)
            summed = jnp.dot(prob, vm[h], preferred_element_type=F32)
            result = summed * (1.0 / summed[:, spare : spare + 1])
            n = w // 128
            tiles[n] = jnp.where(mask[:, :128], result[:, :128], tiles[n])
            tiles[n + 1] = jnp.where(mask[:, 128:], result[:, 128:], tiles[n + 1])
        first = core == 0
        whole = [jnp.where(first, tiles[n], tiles[n + 1]).astype(BF) for n in range(2)]
        shared = jnp.where(first, tiles[2], tiles[0])
        packed = shared[:128] + pltpu.roll(shared[128:], 64, 1)
        packed = packed.astype(BF).reshape(4, 2, 16, 128)
        for g in range(2):
            for n in range(2):
                att[4 * g + t, 8 * n : 8 * n + 8] = whole[n].reshape(8, 2, 16, 128)[:, g]
            att[4 * g + t, 16:] = packed[:, g]
        send4((1 - zh) * 4 + t)
        send4(zh * 4 + t)
        return carry

    lax.fori_loop(0, 4, space_attend, 0)

    def done2(f, carry):
        device = target2(rem(f, 16))

        @pl.when(not_me(device))
        def _():
            pltpu.make_async_remote_copy(
                src_ref=mixed.at[f], dst_ref=tok2.at[f], send_sem=s2.at[f], recv_sem=r2.at[f],
                device_id=device, device_id_type=MESH,
            ).wait_send()

        return carry

    def done3(n, carry):
        exchange_time(div(n, 2), rem(n, 2)).wait_send()
        exchange(n, 0).wait_send()
        exchange(n, 1).wait_send()
        return carry

    def done4(g, carry):
        device = target4(g)

        @pl.when(not_me(device))
        def _():
            pltpu.make_async_remote_copy(
                src_ref=att.at[g], dst_ref=home.at[0], send_sem=s4.at[g], recv_sem=r4.at[0],
                device_id=device, device_id_type=MESH,
            ).wait_send()

        return carry

    lax.fori_loop(16, 32, sent1, 0)
    lax.fori_loop(0, 32, done2, 0)
    lax.fori_loop(0, 4, done3, 0)
    lax.fori_loop(0, 8, done4, 0)

    def arrived(i, carry):
        wait_local(home.at[i], home.at[i], r4.at[i])
        return carry

    lax.fori_loop(0, 8, arrived, 0)


def assemble(home_hbm, out_hbm, home, out, arrive, leave):
    def place(blocks, core, at):
        for n in range(4):
            row = (n // 2 * 4 + n % 2 * 2 + core) * 16
            out[i, 0, row : row + 16, at : at + 128] = blocks[n]

    left = lax.broadcasted_iota(jnp.int32, (1, 128), 1) < 64
    copies = [
        pltpu.make_async_copy(home_hbm.at[pl.ds(2 * i, 2)], home.at[pl.ds(2 * i, 2)], arrive.at[i])
        for i in range(4)
    ]
    results = [pltpu.make_async_copy(out.at[i], out_hbm.at[i], leave.at[i]) for i in range(4)]
    for copy in copies:
        copy.start()
    for i in range(4):
        copies[i].wait()
        for core in range(2):
            for half in range(2):
                for n in range(2):
                    place(home[2 * i + half, 8 * n + 4 * core : 8 * n + 4 * core + 4], core, (3 * half + n) * 128)
        low = home[2 * i, 16:].reshape(64, 128).astype(F32)
        high = home[2 * i + 1, 16:].reshape(64, 128).astype(F32)
        place(jnp.where(left, low, high).astype(BF).reshape(4, 16, 128), 0, 256)
        rolled = pltpu.roll(jnp.where(left, high, low), 64, 1)
        place(rolled.astype(BF).reshape(4, 16, 128), 1, 256)
        results[i].start()
    for result in results:
        result.wait()


def body(
    clip, norm_time, w_time_qkv, q_gain_time, k_gain_time, w_time_out,
    norm_space, w_space_qkv, q_gain_space, k_gain_space,
):
    anywhere = pl.BlockSpec(memory_space=pl.ANY)
    vmem = pl.BlockSpec(memory_space=pltpu.VMEM)
    dma = pltpu.SemaphoreType.DMA
    home = pl.pallas_call(
        kernel,
        out_shape=jax.ShapeDtypeStruct((8, 20, 16, 128), BF),
        in_specs=[anywhere, vmem, anywhere, vmem, vmem, anywhere, vmem, anywhere, vmem, vmem],
        out_specs=anywhere,
        scratch_shapes=[
            pltpu.VMEM((D, 3 * INNER), BF),
            pltpu.VMEM((INNER, D), BF),
            pltpu.VMEM((D, 3 * INNER), BF),
            pltpu.VMEM((INNER, INNER), BF),
            pltpu.VMEM((128, 256), BF),
            pltpu.VMEM((128, 128), BF),
            pltpu.VMEM((32, 16, D), BF),
            pltpu.VMEM((2, 128, INNER), BF),
            pltpu.VMEM((2, 2, 2, 2, 128, INNER), BF),
            pltpu.VMEM((2, 128, INNER), BF),
            pltpu.VMEM((32, 16, D), BF),
            pltpu.VMEM((32, 16, D), BF),
            pltpu.VMEM((4, 3, 2, 4, 16, HALF), BF),
            pltpu.VMEM((2, 4, 3, 2, 4, 16, HALF), BF),
            pltpu.VMEM((4, 1024, 256), BF),
            pltpu.VMEM((8, 20, 16, 128), BF),
            dma((3,)),
            dma((32,)), dma((32,)),
            dma((2, 2)), dma((2, 2)),
            dma((32,)), dma((32,)),
            dma((4, 2)), dma((4, 2)),
            dma((8,)), dma((8,)),
        ],
        compiler_params=pltpu.CompilerParams(
            collective_id=0, has_side_effects=True, vmem_limit_bytes=58 * 2**20
        ),
        cost_estimate=pl.CostEstimate(
            flops=2 * 512 * D * (6 * INNER + INNER), bytes_accessed=14 * 2**20, transcendentals=6 * 2**20
        ),
    )(
        clip, norm_time, w_time_qkv, q_gain_time, k_gain_time, w_time_out,
        norm_space, w_space_qkv, q_gain_space, k_gain_space,
    )
    return pl.pallas_call(
        assemble,
        out_shape=jax.ShapeDtypeStruct((4, 1, 128, INNER), BF),
        in_specs=[anywhere],
        out_specs=anywhere,
        scratch_shapes=[
            pltpu.VMEM((8, 20, 16, 128), BF),
            pltpu.VMEM((4, 1, 128, INNER), BF),
            dma((4,)), dma((4,)),
        ],
    )(home)


def solution(mesh):
    in_specs = (P(None, "frame", "patch", None),) + (P(),) * 9
    out_specs = P(None, "frame", "patch", None)
    return jax.shard_map(body, mesh=mesh, in_specs=in_specs, out_specs=out_specs, check_vma=False)
```

```python
import math

import jax
import jax.numpy as jnp
from jax import lax
from jax.experimental import pallas as pl
from jax.experimental.pallas import tpu as pltpu
from jax.sharding import PartitionSpec as P

MESH = pl.DeviceIdType.MESH
HDIM = 80
HEADS = 8
D = 1280
INNER = 640
HALF = 384
EPS = 1e-06
SCALE = HDIM ** (-0.5) * math.log2(math.e)
BF = jnp.bfloat16
F32 = jnp.float32
WINDOWS = (0, 0, 128, 128, 256, 256, 384, 384)


def div(a, b):
    return lax.div(a, jnp.int32(b))


def rem(a, b):
    return lax.rem(a, jnp.int32(b))


def kernel(
    clip, norm_t, w_tqkv, qg_t, kg_t, w_out, norm_s, w_sqkv, qg_s, kg_s,
    home,
    wt, wo, ws, blocks, pmask, swap, tok, tq, tkv, tatt, mixed, tok2, send_qkv, qkv, vm, att,
    wsem, s1, r1, st, rt, s2, r2, sq, rq, s4, r4,
):
    frame, patch = lax.axis_index("frame"), lax.axis_index("patch")
    x, zl, core = div(frame, 8), rem(div(frame, 2), 4), rem(frame, 2)
    zh, y = div(patch, 4), rem(patch, 4)
    z = zh * 4 + zl
    c, zb = div(z, 2), rem(z, 2)

    def flip(zz, cc):
        return rem(zz + 1 + rem(div(cc + 1, 2), 2), 2)

    zh_src = flip(zb, c)
    pg_src = zh_src * 4 + y

    def is_me(device):
        return (device[0] == frame) & (device[1] == patch)

    def not_me(device):
        return (device[0] != frame) | (device[1] != patch)

    def target1(i):
        xt = rem(x + zl + 4 - div(rem(i, 16), 4), 4)
        ct = rem(c + 1 + i, 4)
        zt = 2 * ct + flip(zh, ct)
        device = (xt * 8 + rem(zt, 4) * 2 + core, div(zt, 4) * 4 + y)
        return device, ct, div(i, 16) * 4 + xt

    def source1(i):
        return (i * 2 + core, pg_src)

    def target2(m):
        zt = 2 * c + core
        yt = rem(rem(m, 4) + c + 2 * core, 4)
        return (div(m, 4) * 8 + rem(zt, 4) * 2 + rem(x, 2), div(zt, 4) * 4 + yt)

    def order2(i):
        xt = rem(x + 1 + 2 * div(i, 8) + rem(i, 2), 4)
        return xt * 4 + rem(div(i, 2) + x + y, 4)

    def source2(i):
        xs, zs = 2 * div(i, 8) + core, 2 * c + rem(i, 2)
        return (xs * 8 + rem(zs, 4) * 2 + zb, div(zs, 4) * 4 + rem(div(i, 2), 4))

    home_zl = rem(y + 8 - c - 2 * zb, 4)
    home_frame = x * 8 + home_zl * 2 + zb

    def target4(g):
        return (home_frame, g)

    def source4(i):
        zs = 2 * div(i, 2) + core
        return (x * 8 + rem(zs, 4) * 2 + rem(i, 2), div(zs, 4) * 4 + rem(zl + div(i, 2) + 2 * core, 4))

    partner = (x * 8 + zl * 2 + 1 - core, patch)

    loads = (
        pltpu.make_async_copy(w_tqkv, wt, wsem.at[0]),
        pltpu.make_async_copy(w_out, wo, wsem.at[1]),
        pltpu.make_async_copy(w_sqkv, ws, wsem.at[2]),
    )
    loads[0].start()
    loads[1].start()
    loads[2].start()

    barrier = pltpu.get_barrier_semaphore()

    def greet(device):
        @pl.when(not_me(device))
        def _():
            pl.semaphore_signal(barrier, inc=1, device_id=device, device_id_type=MESH)

    def greet1(i, carry):
        greet(source1(i))
        return carry

    def greet2(i, carry):
        greet(source2(i))
        return carry

    def greet4(i, carry):
        greet(source4(i))
        return carry

    lax.fori_loop(0, 16, greet1, 0, unroll=True)
    lax.fori_loop(0, 16, greet2, 0, unroll=True)
    lax.fori_loop(0, 8, greet4, 0, unroll=True)
    greet(partner)

    own1 = jnp.where(zh_src == zh, 1, 0)
    own4 = jnp.where(home_frame == frame, 1, 0)
    own2 = jnp.where((core == zb) & (core == rem(x, 2)), 1, 0)
    pl.semaphore_wait(barrier, 16 - own1 + 16 - own2 + 8 - own4 + 1)

    def copy1(i):
        device, ct, b = target1(i)
        src = clip.at[ct, 0, pl.ds(pl.multiple_of(b * 16, 16), 16)]
        return device, src

    def send1(i, carry):
        device, src = copy1(i)
        slot = div(i, 16) * 16 + div(frame, 2)

        @pl.when(not_me(device))
        def _():
            pltpu.make_async_remote_copy(
                src_ref=src, dst_ref=tok.at[slot], send_sem=s1.at[i], recv_sem=r1.at[slot],
                device_id=device, device_id_type=MESH,
            ).start()

        @pl.when(is_me(device))
        def _():
            pltpu.make_async_copy(src, tok.at[slot], r1.at[slot]).start()

        return carry

    def sent1(i, carry):
        device, src = copy1(i)

        @pl.when(not_me(device))
        def _():
            pltpu.make_async_remote_copy(
                src_ref=src, dst_ref=tok.at[0], send_sem=s1.at[i], recv_sem=r1.at[0],
                device_id=device, device_id_type=MESH,
            ).wait_send()

        return carry

    lax.fori_loop(0, 16, send1, 0, unroll=True)

    rows = lax.broadcasted_iota(jnp.int32, (INNER, INNER), 0)
    cols = lax.broadcasted_iota(jnp.int32, (INNER, INNER), 1)
    head_of = lambda v: lax.shift_right_logical(v * 52429, 22)
    blocks[...] = jnp.where(head_of(rows) == head_of(cols), 1.0, 0.0).astype(BF)
    rows = lax.broadcasted_iota(jnp.int32, (128, 256), 0)
    cols = lax.broadcasted_iota(jnp.int32, (128, 256), 1)
    pmask[...] = jnp.where(((rows >> 3) & 7) == ((cols >> 3) & 7), 1.0, 0.0).astype(BF)
    rows = lax.broadcasted_iota(jnp.int32, (128, 128), 0)
    cols = lax.broadcasted_iota(jnp.int32, (128, 128), 1)
    swap[...] = jnp.where(cols == (rows & 7) * 16 + (rows >> 3), 1.0, 0.0).astype(BF)

    def layer_norm(values, gain):
        average = jnp.mean(values, axis=-1, keepdims=True)
        centred = values - average
        variance = jnp.mean(centred * centred, axis=-1, keepdims=True)
        return (centred * lax.rsqrt(variance + EPS) * gain).astype(BF)

    def head_norm(part, gain):
        squares = jnp.dot((part * part).astype(BF), blocks[...], preferred_element_type=F32)
        return (part * lax.rsqrt(squares * (1.0 / HDIM) + EPS) * gain).astype(BF)

    def queries(normed, weight, gain):
        product = jnp.dot(normed, weight[:, :INNER], preferred_element_type=F32)
        return head_norm(product, gain[...].reshape(1, -1))

    def keys_values(normed, weight, gain):
        product = jnp.dot(normed, weight[:, INNER:], preferred_element_type=F32)
        return head_norm(product[:, :INNER], gain[...].reshape(1, -1)), product[:, INNER:].astype(BF)

    def wait_local(src, dst, sem):
        pltpu.make_async_copy(src, dst, sem).wait()

    for load in loads:
        load.wait()

    lane = lax.broadcasted_iota(jnp.int32, (1, 256), 1)

    def exchange_time(batch, j):
        return pltpu.make_async_remote_copy(
            src_ref=tkv.at[batch, core, :, j], dst_ref=tkv.at[batch, core, :, j],
            send_sem=st.at[batch, j], recv_sem=rt.at[batch, j],
            device_id=partner, device_id_type=MESH,
        )

    def time_attend(batch, g):
        rows = pl.ds(pl.multiple_of(g * 64, 64), 64)
        tiles = [jnp.zeros((128, 128), F32)] * 5
        for h in range(HEADS):
            w = WINDOWS[h]
            first = h * HDIM - w
            mask = (lane >= first) & (lane < first + HDIM)
            spare = 255 if first + HDIM <= 255 else 0
            query = jnp.where(mask, tq[:, rows, w : w + 256].reshape(128, 256), 0.0).astype(BF)
            keys = tkv[batch, :, 0, :, rows, w : w + 256].reshape(256, 256)
            scores = lax.dot_general(
                query, keys, (((1,), (1,)), ((), ())), preferred_element_type=F32
            )
            prob = jnp.exp2(scores * SCALE).astype(BF) * pmask[...]
            vals = tkv[batch, :, 1, :, rows, w : w + 256].reshape(256, 256)
            vals = jnp.where(mask, vals, 1.0).astype(BF)
            summed = jnp.dot(prob, vals, preferred_element_type=F32)
            result = summed * (1.0 / summed[:, spare : spare + 1])
            t = w // 128
            tiles[t] = jnp.where(mask[:, :128], result[:, :128], tiles[t])
            tiles[t + 1] = jnp.where(mask[:, 128:], result[:, 128:], tiles[t + 1])
        for n in range(5):
            tatt[:, rows, n * 128 : (n + 1) * 128] = tiles[n].astype(BF).reshape(2, 64, 128)

    def send2(batch, m):
        f = batch * 16 + m
        device = target2(m)
        slot = batch * 16 + div(x, 2) * 8 + pg_src

        @pl.when(not_me(device))
        def _():
            pltpu.make_async_remote_copy(
                src_ref=mixed.at[f], dst_ref=tok2.at[slot], send_sem=s2.at[f],
                recv_sem=r2.at[slot], device_id=device, device_id_type=MESH,
            ).start()

        @pl.when(is_me(device))
        def _():
            pltpu.make_async_copy(mixed.at[f], tok2.at[slot], r2.at[slot]).start()

    def time_step(batch, carry):
        @pl.when(batch == 0)
        def _():
            for j in range(2):
                lax.fori_loop(8 * j, 8 * j + 8, sent1, 0, unroll=True)
                lax.fori_loop(8 * j + 16, 8 * j + 24, send1, 0, unroll=True)

        def project(j, inner):
            slots = [
                batch * 16 + a * 4 + rem(x + 2 * j + k + 4 - a, 4) for a in range(4) for k in range(2)
            ]
            for slot in slots:
                wait_local(tok.at[slot], tok.at[slot], r1.at[slot])
            values = jnp.concatenate([tok[slot] for slot in slots], axis=0)
            values = jnp.dot(swap[...], values, preferred_element_type=F32)
            normed = layer_norm(values, norm_t[...].reshape(1, -1))
            for n, part in enumerate(keys_values(normed, wt, kg_t)):
                tkv[batch, core, n, j] = part
            exchange_time(batch, j).start()
            tq[j] = queries(normed, wt, qg_t)
            return inner

        lax.fori_loop(0, 2, project, 0)
        for j in range(2):
            wait_local(tkv.at[batch, core, :, j], tkv.at[batch, 1 - core, :, j], rt.at[batch, j])

        def attend(g, inner):
            time_attend(batch, g)
            return inner

        lax.fori_loop(0, 2, attend, 0, unroll=True)

        def mix(half, inner):
            near = [rem(x + 1 + 2 * half + i, 4) for i in range(2)]
            rows = lax.broadcasted_iota(jnp.int32, (128, 256), 0)
            cols = lax.broadcasted_iota(jnp.int32, (128, 256), 1)
            a = jnp.where(rows < 64, near[0], near[1])
            d = (a + (rows >> 4) + 8 - x) & 3
            source = (d >> 1) * 128 + (rows & 15) * 8 + a * 2 + (d & 1)
            pick = jnp.where(cols == source, 1.0, 0.0).astype(BF)
            attended = tatt[...].reshape(256, INNER)
            attended = jnp.dot(pick, attended, preferred_element_type=F32).astype(BF)
            delta = jnp.dot(attended, wo[...], preferred_element_type=F32)
            for i in range(2):
                at = pl.ds(batch * 16 + near[i] * 4, 4)
                total = (tok[at].reshape(64, D).astype(F32) + delta[64 * i : 64 * i + 64]).astype(BF)
                mixed[at] = total.reshape(4, 16, D)

            def send(i, deeper):
                send2(batch, order2(half * 8 + i))
                return deeper

            lax.fori_loop(0, 8, send, 0, unroll=True)
            return inner

        lax.fori_loop(0, 2, mix, 0, unroll=True)
        return carry

    lax.fori_loop(0, 2, time_step, 0)

    def exchange(n, part):
        which = pl.ds(0, 1) if part == 0 else pl.ds(1, 2)
        return pltpu.make_async_remote_copy(
            src_ref=send_qkv.at[n, which], dst_ref=qkv.at[core, n, which],
            send_sem=sq.at[n, part], recv_sem=rq.at[n, part],
            device_id=partner, device_id_type=MESH,
        )

    def space_step(j, carry):
        early = rem(x + 3 - rem(x + core + 1, 2), 4)
        quarter = div(j, 2) * 2 + rem(div(early, 2) + j, 2)

        def wait(i, inner):
            slot = quarter * 8 + i
            wait_local(tok2.at[slot], tok2.at[slot], r2.at[slot])
            return inner

        lax.fori_loop(0, 8, wait, 0, unroll=True)
        values = tok2[pl.ds(quarter * 8, 8)].reshape(128, D).astype(F32)
        normed = layer_norm(values, norm_s[...].reshape(1, -1))

        def keep(n, part):
            low, high = part[:, :HALF], part[:, INNER - HALF :]
            mine, other = jnp.where(core == 0, low, high), jnp.where(core == 0, high, low)
            qkv[core, quarter, n] = mine.reshape(2, 4, 16, HALF)
            send_qkv[quarter, n] = other.reshape(2, 4, 16, HALF)

        for n, part in enumerate(keys_values(normed, ws, kg_s)):
            keep(1 + n, part)
        exchange(quarter, 1).start()
        keep(0, queries(normed, ws, qg_s))
        exchange(quarter, 0).start()
        return carry

    lax.fori_loop(0, 4, space_step, 0)

    def wait_partner(n, carry):
        for part, which in enumerate((pl.ds(0, 1), pl.ds(1, 2))):
            wait_local(send_qkv.at[n, which], qkv.at[1 - core, n, which], rq.at[n, part])
        return carry

    lax.fori_loop(0, 4, wait_partner, 0, unroll=True)

    def head_mask(j):
        first = j * HDIM + 64 * core - (0 if j < 2 else 128)
        return (lane >= first) & (lane < first + HDIM)

    for j in range(4):
        w = 0 if j < 2 else 128
        vals = qkv[:, :, 2, :, :, :, w : w + 256].reshape(1024, 256)
        vm[j] = jnp.where(head_mask(j), vals, 1.0).astype(BF)

    def send4(g):
        device = target4(g)
        slot = c * 2 + core
        src, dst = att.at[g], home.at[slot]

        @pl.when(not_me(device))
        def _():
            pltpu.make_async_remote_copy(
                src_ref=src, dst_ref=dst, send_sem=s4.at[g], recv_sem=r4.at[slot],
                device_id=device, device_id_type=MESH,
            ).start()

        @pl.when(is_me(device))
        def _():
            pltpu.make_async_copy(src, dst, r4.at[slot]).start()

    def space_attend(j, carry):
        t = rem(y + 1 + j, 4)
        tiles = [jnp.zeros((256, 128), F32)] * 3
        for h in range(4):
            w = 0 if h < 2 else 128
            spare = 255 if h < 2 else 0
            mask = head_mask(h)
            query = qkv[:, :, 0, :, t, :, w : w + 256].reshape(256, 256)
            query = jnp.where(mask, query, 0.0).astype(BF)
            keys = qkv[:, :, 1, :, :, :, w : w + 256].reshape(1024, 256)
            scores = lax.dot_general(
                query, keys, (((1,), (1,)), ((), ())), preferred_element_type=F32
            )
            prob = jnp.exp2(scores * SCALE).astype(BF)
            summed = jnp.dot(prob, vm[h], preferred_element_type=F32)
            result = summed * (1.0 / summed[:, spare : spare + 1])
            n = w // 128
            tiles[n] = jnp.where(mask[:, :128], result[:, :128], tiles[n])
            tiles[n + 1] = jnp.where(mask[:, 128:], result[:, 128:], tiles[n + 1])
        first = core == 0
        whole = [jnp.where(first, tiles[n], tiles[n + 1]).astype(BF) for n in range(2)]
        shared = jnp.where(first, tiles[2], tiles[0])
        packed = shared[:128] + pltpu.roll(shared[128:], 64, 1)
        packed = packed.astype(BF).reshape(4, 2, 16, 128)
        for g in range(2):
            for n in range(2):
                att[4 * g + t, 8 * n : 8 * n + 8] = whole[n].reshape(8, 2, 16, 128)[:, g]
            att[4 * g + t, 16:] = packed[:, g]
        send4((1 - zh) * 4 + t)
        send4(zh * 4 + t)
        return carry

    lax.fori_loop(0, 4, space_attend, 0)

    def done2(f, carry):
        device = target2(rem(f, 16))

        @pl.when(not_me(device))
        def _():
            pltpu.make_async_remote_copy(
                src_ref=mixed.at[f], dst_ref=tok2.at[f], send_sem=s2.at[f], recv_sem=r2.at[f],
                device_id=device, device_id_type=MESH,
            ).wait_send()

        return carry

    def done3(n, carry):
        exchange_time(div(n, 2), rem(n, 2)).wait_send()
        exchange(n, 0).wait_send()
        exchange(n, 1).wait_send()
        return carry

    def done4(g, carry):
        device = target4(g)

        @pl.when(not_me(device))
        def _():
            pltpu.make_async_remote_copy(
                src_ref=att.at[g], dst_ref=home.at[0], send_sem=s4.at[g], recv_sem=r4.at[0],
                device_id=device, device_id_type=MESH,
            ).wait_send()

        return carry

    lax.fori_loop(16, 32, sent1, 0)
    lax.fori_loop(0, 32, done2, 0)
    lax.fori_loop(0, 4, done3, 0)
    lax.fori_loop(0, 8, done4, 0)

    def arrived(i, carry):
        wait_local(home.at[i], home.at[i], r4.at[i])
        return carry

    lax.fori_loop(0, 8, arrived, 0, unroll=True)


def assemble(home_hbm, out_hbm, home, out, arrive, leave):
    def place(blocks, core, at):
        for n in range(4):
            row = (n // 2 * 4 + n % 2 * 2 + core) * 16
            out[i, 0, row : row + 16, at : at + 128] = blocks[n]

    left = lax.broadcasted_iota(jnp.int32, (1, 128), 1) < 64
    copies = [
        pltpu.make_async_copy(home_hbm.at[pl.ds(2 * i, 2)], home.at[pl.ds(2 * i, 2)], arrive.at[i])
        for i in range(4)
    ]
    results = [pltpu.make_async_copy(out.at[i], out_hbm.at[i], leave.at[i]) for i in range(4)]
    for copy in copies:
        copy.start()
    for i in range(4):
        copies[i].wait()
        for core in range(2):
            for half in range(2):
                for n in range(2):
                    place(home[2 * i + half, 8 * n + 4 * core : 8 * n + 4 * core + 4], core, (3 * half + n) * 128)
        low = home[2 * i, 16:].reshape(64, 128).astype(F32)
        high = home[2 * i + 1, 16:].reshape(64, 128).astype(F32)
        place(jnp.where(left, low, high).astype(BF).reshape(4, 16, 128), 0, 256)
        rolled = pltpu.roll(jnp.where(left, high, low), 64, 1)
        place(rolled.astype(BF).reshape(4, 16, 128), 1, 256)
        results[i].start()
    for result in results:
        result.wait()


def body(
    clip, norm_time, w_time_qkv, q_gain_time, k_gain_time, w_time_out,
    norm_space, w_space_qkv, q_gain_space, k_gain_space,
):
    anywhere = pl.BlockSpec(memory_space=pl.ANY)
    vmem = pl.BlockSpec(memory_space=pltpu.VMEM)
    dma = pltpu.SemaphoreType.DMA
    home = pl.pallas_call(
        kernel,
        out_shape=jax.ShapeDtypeStruct((8, 20, 16, 128), BF),
        in_specs=[anywhere, vmem, anywhere, vmem, vmem, anywhere, vmem, anywhere, vmem, vmem],
        out_specs=anywhere,
        scratch_shapes=[
            pltpu.VMEM((D, 3 * INNER), BF),
            pltpu.VMEM((INNER, D), BF),
            pltpu.VMEM((D, 3 * INNER), BF),
            pltpu.VMEM((INNER, INNER), BF),
            pltpu.VMEM((128, 256), BF),
            pltpu.VMEM((128, 128), BF),
            pltpu.VMEM((32, 16, D), BF),
            pltpu.VMEM((2, 128, INNER), BF),
            pltpu.VMEM((2, 2, 2, 2, 128, INNER), BF),
            pltpu.VMEM((2, 128, INNER), BF),
            pltpu.VMEM((32, 16, D), BF),
            pltpu.VMEM((32, 16, D), BF),
            pltpu.VMEM((4, 3, 2, 4, 16, HALF), BF),
            pltpu.VMEM((2, 4, 3, 2, 4, 16, HALF), BF),
            pltpu.VMEM((4, 1024, 256), BF),
            pltpu.VMEM((8, 20, 16, 128), BF),
            dma((3,)),
            dma((32,)), dma((32,)),
            dma((2, 2)), dma((2, 2)),
            dma((32,)), dma((32,)),
            dma((4, 2)), dma((4, 2)),
            dma((8,)), dma((8,)),
        ],
        compiler_params=pltpu.CompilerParams(
            collective_id=0, has_side_effects=True, vmem_limit_bytes=58 * 2**20
        ),
        cost_estimate=pl.CostEstimate(
            flops=2 * 512 * D * (6 * INNER + INNER), bytes_accessed=14 * 2**20, transcendentals=6 * 2**20
        ),
    )(
        clip, norm_time, w_time_qkv, q_gain_time, k_gain_time, w_time_out,
        norm_space, w_space_qkv, q_gain_space, k_gain_space,
    )
    return pl.pallas_call(
        assemble,
        out_shape=jax.ShapeDtypeStruct((4, 1, 128, INNER), BF),
        in_specs=[anywhere],
        out_specs=anywhere,
        scratch_shapes=[
            pltpu.VMEM((8, 20, 16, 128), BF),
            pltpu.VMEM((4, 1, 128, INNER), BF),
            dma((4,)), dma((4,)),
        ],
    )(home)


def solution(mesh):
    in_specs = (P(None, "frame", "patch", None),) + (P(),) * 9
    out_specs = P(None, "frame", "patch", None)
    return jax.shard_map(body, mesh=mesh, in_specs=in_specs, out_specs=out_specs, check_vma=False)
```
